128 devices in a mesh: row: 16 (over z, x), col: 8 (over y, core).
Axes of the slice: x: 4, y: 4, z: 4, core: 2. Of those that a mesh axis runs over, the one named last changes fastest.
Arguments:
- right_sides: bfloat16 [31, 2432, 256], P(None, ('row', 'col')), may hold values from -6 to 6
- lower_inv: bfloat16 [31, 2432, 2432], P(None, 'col', 'row'), as said below
- lower_off: bfloat16 [98, 2432, 2432], P(None, 'row', 'col'), may hold values from -0.0625 to 0.0625
- upper_inv: bfloat16 [31, 2432, 2432], P(None, 'row', 'col'), as said below
- upper_off: bfloat16 [98, 2432, 2432], P(None, 'col', 'row'), may hold values from -0.0625 to 0.0625
- present: int32 [98], replicated, may hold values 0 or 1
Outputs:
- solution: float32 [31, 2432, 256], P(None, ('row', 'col'))
The draws below stay inside these ranges and needn't reach their ends.
Inputs may be any that keep to these rules, and one draw needn't show every extreme that they name: `lower_inv`: each block is unit lower triangular. `upper_inv`: each block is upper triangular with a positive diagonal.
All inputs are finite; a program needn't handle non-finite values.
Results may differ from the reference program's by a relative error of at most 0.034.
Values may be sent and summed in bfloat16 or wider, within the bound.
A program may use at most 128 MiB of HBM per device.

```python
import math
import jax
import jax.numpy as jnp
from jax import lax

W = 2432
LEVELS = 5
R = 256
K = 31
NOFF = 98


def draw_lower_inv(key, part):
    key = jax.random.fold_in(key, 11)
    rows_idx = lax.broadcasted_iota(jnp.int32, (K, W, W), 1)
    cols_idx = lax.broadcasted_iota(jnp.int32, (K, W, W), 2)
    noise = jax.random.normal(key, (K, W, W), jnp.float32) * (1.0 / math.sqrt(W))
    identity = jnp.where(rows_idx == cols_idx, 1.0, 0.0).astype(jnp.float32)
    return (identity + jnp.where(rows_idx > cols_idx, noise, 0.0)).astype(jnp.bfloat16)


def draw_upper_inv(key, part):
    key = jax.random.fold_in(key, 23)
    rows_idx = lax.broadcasted_iota(jnp.int32, (K, W, W), 1)
    cols_idx = lax.broadcasted_iota(jnp.int32, (K, W, W), 2)
    noise = jax.random.normal(key, (K, W, W), jnp.float32) * (1.0 / math.sqrt(W))
    pivots = jax.random.uniform(jax.random.fold_in(key, 7), (K, W, W), jnp.float32, 0.5, 2.0)
    result = jnp.where(rows_idx == cols_idx, pivots, jnp.where(rows_idx < cols_idx, noise, 0.0))
    return result.astype(jnp.bfloat16)


def place_ends(values, stream_key, least, top_value):
    longest = values.shape.index(max(values.shape))
    spots = []
    for shift in (0, 1):
        where = [jax.random.randint(jax.random.fold_in(stream_key, axis), (), 0, length) for axis, length in enumerate(values.shape)]
        where[longest] = (where[longest] + shift) % values.shape[longest]
        spots.append(tuple(where))
    return values.at[spots[0]].set(least).at[spots[1]].set(top_value)


def levels(rng, dims, pieces, smallest, largest):
    level = 1.0
    for dim, parts in pieces:
        draws = jax.random.uniform(jax.random.fold_in(jax.random.fold_in(rng, 6), dim), (parts,), jnp.float32, smallest / len(pieces), largest / len(pieces))
        level = level * jnp.repeat(jnp.exp(draws), dims[dim] // parts).reshape((-1,) + (1,) * (len(dims) - 1 - dim))
    return level


def normal_values(own_key, extent, scale, reach, shards=(), held_as=jnp.bfloat16):
    gain = levels(own_key, extent, shards, -0.22, 0.18) if shards else 1.0
    array = jax.random.normal(own_key, extent, jnp.float32) * scale * gain
    return jnp.minimum(jnp.maximum(array, -reach), reach).astype(held_as)


def setup_inputs(seed: int = 0) -> dict:
    seeds = jax.random.split(jax.random.key(seed), 7)
    right_sides = normal_values(seeds[0], (K, W, R), 1.0, 6.0, ((1, 128),))
    lower_inv = draw_lower_inv(jax.random.fold_in(seeds[6], 71), 0)
    lower_off = normal_values(seeds[2], (NOFF, W, W), (4 * W) ** -0.5, 0.0625, ((1, 16), (2, 8)))
    upper_inv = draw_upper_inv(jax.random.fold_in(seeds[6], 71), 0)
    upper_off = normal_values(seeds[4], (NOFF, W, W), (4 * W) ** -0.5, 0.0625, ((1, 8), (2, 16)))
    present = place_ends((jax.random.randint(seeds[5], (NOFF,), 0, 4) < 3).astype(jnp.int32), jax.random.fold_in(seeds[5], 1), 0, 1)
    return dict(right_sides=right_sides, lower_inv=lower_inv, lower_off=lower_off, upper_inv=upper_inv, upper_off=upper_off, present=present)


def level_layout():
    first_nodes = []
    first_blocks = []
    node_total = 0
    block_total = 0
    for height in range(LEVELS):
        members = 2 ** (LEVELS - 1 - height)
        first_nodes.append(node_total)
        first_blocks.append(block_total)
        node_total += members
        block_total += members * (LEVELS - 1 - height)
    return first_nodes, first_blocks


def reference(right_sides, lower_inv, lower_off, upper_inv, upper_off, present):
    first_nodes, first_blocks = level_layout()
    block_scale = present.astype(jnp.float32)
    waiting_nodes = [jnp.zeros((W, R), jnp.float32) for node_number in range(K)]
    forward = [None] * K
    for height in range(LEVELS):
        members = 2 ** (LEVELS - 1 - height)
        ancestors = LEVELS - 1 - height
        for member in range(members):
            node_number = first_nodes[height] + member
            lowered = (right_sides[node_number].astype(jnp.float32) - waiting_nodes[node_number]).astype(jnp.bfloat16)
            solved_part = jnp.dot(lower_inv[node_number], lowered, preferred_element_type=jnp.float32)
            forward[node_number] = solved_part
            rounded = solved_part.astype(jnp.bfloat16)
            for tree_distance in range(1, ancestors + 1):
                block_number = first_blocks[height] + member * ancestors + tree_distance - 1
                target = first_nodes[height + tree_distance] + (member >> tree_distance)
                waiting_nodes[target] = waiting_nodes[target] + block_scale[block_number] * jnp.dot(lower_off[block_number], rounded, preferred_element_type=jnp.float32)
    upward = [jnp.zeros((W, R), jnp.float32) for node_number in range(K)]
    results = [None] * K
    for height in reversed(range(LEVELS)):
        members = 2 ** (LEVELS - 1 - height)
        for member in range(members):
            node_number = first_nodes[height] + member
            raised = (forward[node_number] - upward[node_number]).astype(jnp.bfloat16)
            solved_part = jnp.dot(upper_inv[node_number], raised, preferred_element_type=jnp.float32)
            results[node_number] = solved_part
            rounded = solved_part.astype(jnp.bfloat16)
            for tree_distance in range(1, height + 1):
                lower_height = height - tree_distance
                lower_above = LEVELS - 1 - lower_height
                for offspring in range(member << tree_distance, (member + 1) << tree_distance):
                    block_number = first_blocks[lower_height] + offspring * lower_above + tree_distance - 1
                    target = first_nodes[lower_height] + offspring
                    upward[target] = upward[target] + block_scale[block_number] * jnp.dot(upper_off[block_number], rounded, preferred_element_type=jnp.float32)
    return jnp.stack(results, axis=0)
```

```python
import jax
import jax.numpy as jnp
import numpy as np
from jax import lax
from jax.experimental import pallas as pl
from jax.experimental.pallas import tpu as pltpu
from jax.sharding import PartitionSpec as P

LEVELS = 5
K = 31
NOFF = 98
R = 256
H = 128
TALL = 304
LOW = 152
PITCH = 160
SMALL = 19
PAIR = 48
MEMBERS = [16, 8, 4, 2, 1]
NODE = [0, 16, 24, 28, 30]
SLOT = [0, 64, 88, 96, 98]
PIECE = {16: 1216, 8: 608, 4: 304, 2: 160, 1: 80}
CHUNK = {16: 304, 8: 304, 4: 304, 2: 160, 1: 80}
FWROW = [0, 1216, 1824, 2128, 2288]
FWROWS = 2368
MESH = pl.DeviceIdType.MESH
BF = jnp.bfloat16
F32 = jnp.float32

RS, EX, AG, CR, CG, YX, IY, IC, FC, FY = 0, 6, 12, 18, 19, 20, 26, 32, 34, 35
NSEM = 38


def placing():
    put = np.zeros((2, LOW, 8 * PAIR), np.float32)
    for r in range(LOW):
        c, i = divmod(r, SMALL)
        at = ((c % 2) * 4 + c // 2) * PAIR + i
        put[0, r, at] = 1
        put[1, r, at + SMALL] = 1
    return put, np.swapaxes(put, 1, 2)


def dot(a, b):
    return jnp.dot(a, b, preferred_element_type=F32)


def kernel(
    rs, put, take, present, linv, loff, uinv, uoff, out,
    pb, rb, es, eb, xb, fw, tot, cb, crb, ct, ys, yb, lowb, rg, ag0, ag1, sp, crs, fys, fyr,
    ssem, rsem, wsem,
):
    row, col = lax.axis_index("row"), lax.axis_index("col")
    z, x = row // 4, row % 4
    y, core = col // 2, col % 2
    sibling = (row, y * 2 + 1 - core)
    along = (z, x)

    def zpeer(d):
        return (((z + d) % 4) * 4 + x, col)

    def xpeer(d):
        return (z * 4 + (x + d) % 4, col)

    def ypeer(d):
        return (row, ((y + d) % 4) * 2 + core)

    first_peer = (zpeer, xpeer)
    second_peer = (xpeer, zpeer)

    barrier = pltpu.get_barrier_semaphore()
    for d in (1, 2, 3):
        for peer in (zpeer, xpeer, ypeer):
            pl.semaphore_signal(barrier, inc=1, device_id=peer(d), device_id_type=MESH)
    pl.semaphore_signal(barrier, inc=1, device_id=sibling, device_id_type=MESH)
    pl.semaphore_wait(barrier, 10)

    def send(src, dst, sem, to):
        c = pltpu.make_async_remote_copy(
            src, dst, ssem.at[sem], rsem.at[sem], device_id=to, device_id_type=MESH
        )
        c.start()
        return c

    def wait(copies):
        for c in copies:
            c.wait()

    def chunks(rows, chunk, body):
        if rows == chunk:
            body(pl.ds(0, chunk), 0)
        else:

            def step(i, _):
                at = pl.multiple_of(i * chunk, 16)
                body(pl.ds(at, chunk), at)
                return 0

            lax.fori_loop(0, rows // chunk, step, 0)

    def each(n, body):
        if n <= 2:
            for i in range(n):
                body(i)
        else:

            def step(i, _):
                body(i)
                return 0

            lax.fori_loop(0, n, step, 0)

    def tall_get(ref, m, j):
        if m >= 4:
            per = m // 4
            q, at = j // per, (j % per) * TALL
            if not isinstance(at, int):
                at = pl.multiple_of(at, 16)
            halves = [ref[h, q, pl.ds(at, TALL), :] for h in (0, 1)]
        elif m == 2:
            halves = [
                jnp.concatenate([ref[h, 2 * j, 0:160, :], ref[h, 2 * j + 1, 0:144, :]], axis=0)
                for h in (0, 1)
            ]
        else:
            halves = [
                jnp.concatenate(
                    [ref[h, q, 0:80, :] for q in range(3)] + [ref[h, 3, 0:64, :]], axis=0
                )
                for h in (0, 1)
            ]
        return jnp.concatenate(halves, axis=1)

    def tall_put(ref, m, j, value):
        value = value.astype(BF)
        for h in (0, 1):
            v = value[:, h * H : (h + 1) * H]
            if m >= 4:
                per = m // 4
                q, at = j // per, (j % per) * TALL
                if not isinstance(at, int):
                    at = pl.multiple_of(at, 16)
                ref[h, q, pl.ds(at, TALL), :] = v
            elif m == 2:
                ref[h, 2 * j, 0:160, :] = v[0:160]
                ref[h, 2 * j + 1, 0:144, :] = v[160:304]
            else:
                for q in range(3):
                    ref[h, q, 0:80, :] = v[80 * q : 80 * q + 80]
                ref[h, 3, 0:64, :] = v[240:304]

    def low_rows(j):
        at = j * PITCH
        return pl.ds(at if isinstance(at, int) else pl.multiple_of(at, 16), LOW)

    def low_get(ref, j):
        return jnp.concatenate([ref[h, low_rows(j), :] for h in (0, 1)], axis=1)

    def low_put(ref, j, value):
        value = value.astype(BF)
        for h in (0, 1):
            ref[h, low_rows(j), :] = value[:, h * H : (h + 1) * H]

    def row_start(rows):
        return [
            [
                send(
                    pb.at[h, (along[h] + d) % 4, pl.ds(0, rows)],
                    rb.at[h, d - 1, pl.ds(0, rows)],
                    RS + h * 3 + d - 1,
                    first_peer[h](d),
                )
                for d in (2, 1, 3)
            ]
            for h in (0, 1)
        ]

    def row_finish(copies, level, forward, aside=None):
        m = MEMBERS[level]
        rows, chunk, base = PIECE[m], CHUNK[m], FWROW[level]
        second = []
        for h in (0, 1):
            wait(copies[h])

            def add(at, _, h=h):
                s = pb[h, along[h], at, :].astype(F32)
                for k in range(3):
                    s = s + rb[h, k, at, :].astype(F32)
                tot[h, at, :] = s
                es[h, at, :] = s.astype(BF)

            chunks(rows, chunk, add)
            second.append(
                [
                    send(
                        es.at[h, pl.ds(0, rows)],
                        eb.at[h, d - 1, pl.ds(0, rows)],
                        EX + h * 3 + d - 1,
                        second_peer[h](d),
                    )
                    for d in (2, 1, 3)
                ]
            )
        if aside is not None:
            aside()
        third = []
        for h in (0, 1):
            wait(second[h])

            def last(at, start, h=h):
                s = tot[h, at, :]
                for k in range(3):
                    s = s + eb[h, k, at, :].astype(F32)
                kept = pl.ds(
                    base + start if isinstance(start, int) else pl.multiple_of(base + start, 16),
                    chunk,
                )
                if forward:
                    fw[h, kept, :] = s
                else:
                    s = fw[h, kept, :] - s
                xb[h, along[h], at, :] = s.astype(BF)

            chunks(rows, chunk, last)
            mine = xb.at[h, along[h], pl.ds(0, rows)]
            third.append(
                [send(mine, mine, AG + h * 3 + d - 1, first_peer[h](d)) for d in (2, 1, 3)]
            )
        for h in (0, 1):
            wait(third[h])

    def col_reduce(m, turn, base=None, aside=None):
        rows = m * PITCH
        wait([send(cb.at[1 - core, pl.ds(0, rows)], crb.at[pl.ds(0, rows)], CR, sibling)])

        def add(at, _):
            s = cb[core, at, :].astype(F32) + crb[at, :].astype(F32)
            ct[at, :] = s
            ys[at, :] = s.astype(BF)

        chunks(rows, PITCH, add)
        copies = [
            send(
                ys.at[pl.ds(0, rows)],
                yb.at[turn, d - 1, pl.ds(0, rows)],
                YX + turn * 3 + d - 1,
                ypeer(d),
            )
            for d in (2, 1, 3)
        ]
        if aside is not None:
            aside()
        wait(copies)

        def last(at, start):
            s = ct[at, :]
            for k in range(3):
                s = s + yb[turn, k, at, :].astype(F32)
            if base is not None:
                first = base + start
                if not isinstance(start, int):
                    first = pl.multiple_of(first, 16)
                s = rg[core, pl.ds(first, PITCH), :].astype(F32) - s
            lowb[core, at, :] = s.astype(BF)

        chunks(rows, PITCH, last)
        mine = lowb.at[core, pl.ds(0, rows)]
        wait([send(mine, mine, CG, sibling)])

    def gather_y(part, buf):
        return [
            send(rs.at[part], buf.at[core, y], IY + part * 3 + d - 1, ypeer(d)) for d in (2, 1, 3)
        ]

    def unpack(buf, pairs, into, single_last):
        def one(p):
            at = p * PAIR
            if not isinstance(at, int):
                at = pl.multiple_of(at, 16)
            v = buf[:, :, pl.ds(at, PAIR), :].reshape(8 * PAIR, R)
            for e in (0, 1):
                low_put(into, 2 * p + e, dot(put[e], v))

        each(pairs - 1 if single_last else pairs, one)
        if single_last:
            p = pairs - 1
            v = buf[:, :, pl.ds(p * PAIR, PAIR), :].reshape(8 * PAIR, R)
            low_put(into, 2 * p, dot(put[0], v))

    turn = 0

    def fetch(src, dst, first, n, sem):
        c = pltpu.make_async_copy(src.at[pl.ds(first, n)], dst.at[pl.ds(first, n)], wsem.at[sem])
        c.start()
        return c

    def forward_sweep(li, lo, waiting):
        inv_copy, off_copy = [], []
        ic0 = gather_y(0, ag0)
        ic1 = gather_y(1, ag1)
        for level in range(LEVELS):
            inv_copy.append(fetch(linv, li, NODE[level], MEMBERS[level], level))
            if level < 4:
                off_copy.append(
                    fetch(loff, lo, SLOT[level], SLOT[level + 1] - SLOT[level], 5 + level)
                )
        ag0[core, y] = rs[0]
        ag1[core, y] = rs[1]
        wait(ic0)
        wait([send(ag0.at[core], ag0.at[core], IC, sibling)])
        unpack(ag0, 8, lowb, False)
        turn = 0
        for level in range(LEVELS):
            m = MEMBERS[level]
            above = LEVELS - 1 - level
            inv_copy[level].wait()
            each(m, lambda j: tall_put(pb, m, j, dot(li[NODE[level] + j], low_get(lowb, j))))
            copies = row_start(PIECE[m])
            if level == 0:
                wait(ic1)
                wait([send(ag1.at[core], ag1.at[core], IC + 1, sibling)])
                unpack(ag1, 8, rg, True)
                waiting[...] = jnp.zeros_like(waiting)
            row_finish(copies, level, True)
            if above == 0:
                break
            off_copy[level].wait()

            def product(j, a):
                slot = SLOT[level] + j * above + a - 1
                scale = present[slot].astype(F32)
                return scale * dot(lo[slot], tall_get(xb, m, j))

            def near(t):
                value = product(2 * t, 1) + product(2 * t + 1, 1)
                if level > 0:
                    value = value + waiting[NODE[level + 1] - 16 + t]
                low_put(cb, t, value)

            each(m // 2, near)

            def far():
                def one(j):
                    for a in range(2, above + 1):
                        t = NODE[level + a] - 16 + j // 2**a
                        waiting[t] = waiting[t] + product(j, a)

                each(m, one)

            col_reduce(
                m // 2, turn, (NODE[level + 1] - 16) * PITCH, far if above > 1 else None
            )
            turn = 1 - turn

    pl.run_scoped(
        forward_sweep,
        pltpu.VMEM((K, TALL, LOW), BF),
        pltpu.VMEM((NOFF, LOW, TALL), BF),
        pltpu.VMEM((15, LOW, R), F32),
    )

    def backward_sweep(ui, uo, upward):
        inv_copy, off_copy = {}, {}
        for level in reversed(range(LEVELS)):
            if level < 4:
                off_copy[level] = fetch(
                    uoff, uo, SLOT[level], SLOT[level + 1] - SLOT[level], 5 + level
                )
            inv_copy[level] = fetch(uinv, ui, NODE[level], MEMBERS[level], level)
        turn = 0
        for level in reversed(range(1, LEVELS)):
            m = MEMBERS[level]
            inv_copy[level].wait()
            each(m, lambda j: low_put(cb, j, dot(ui[NODE[level] + j], tall_get(xb, m, j))))
            col_reduce(m, turn)
            turn = 1 - turn
            if level == 4:
                off_copy[3].wait()

            def product(j, a):
                under = level - a
                slot = SLOT[under] + j * (LEVELS - 1 - under) + a - 1
                scale = present[slot].astype(F32)
                return scale * dot(uo[slot], low_get(lowb, j // 2**a))

            def near(j):
                value = product(j, 1)
                if level < 4:
                    value = value + upward[NODE[level - 1] + j]
                tall_put(pb, 2 * m, j, value)

            each(2 * m, near)
            copies = row_start(PIECE[2 * m])
            for a in range(2, level + 1):
                under = level - a
                if level == 4:
                    off_copy[under].wait()

                def far(j, a=a, under=under):
                    value = product(j, a)
                    if level < 4:
                        value = value + upward[NODE[under] + j]
                    upward[NODE[under] + j] = value

                each(MEMBERS[under], far)
            own = pl.ds(pl.multiple_of((core * 4 + y) * PAIR, 16), PAIR)
            if m == 1:
                out[15] = dot(take[0, own, :], low_get(lowb, 0))
            else:

                def show(p):
                    out[NODE[level] // 2 + p] = dot(
                        take[0, own, :], low_get(lowb, 2 * p)
                    ) + dot(take[1, own, :], low_get(lowb, 2 * p + 1))

                each(m // 2, show)
            row_finish(copies, level - 1, False)

        inv_copy[0].wait()

        def leaf(p):
            at = pl.multiple_of(p * PAIR, 16)
            v = [
                dot(ui[2 * p + e], tall_get(xb, 16, 2 * p + e)).astype(BF) for e in (0, 1)
            ]
            s = dot(take[0], v[0]) + dot(take[1], v[1])
            sp[:, :, pl.ds(at, PAIR), :] = s.astype(BF).reshape(2, 4, PAIR, R)

        each(8, leaf)
        wait([send(sp.at[1 - core], crs, FC, sibling)])
        copies = []
        for d in (2, 1, 3):
            to = (y + d) % 4

            def add(at, _, to=to):
                fys[to, at, :] = (
                    sp[core, to, at, :].astype(F32) + crs[to, at, :].astype(F32)
                ).astype(BF)

            chunks(8 * PAIR, 2 * PAIR, add)
            copies.append(send(fys.at[to], fyr.at[d - 1], FY + d - 1, ypeer(d)))
        wait(copies)

        def finish(p):
            at = pl.ds(pl.multiple_of(p * PAIR, 16), PAIR)
            s = sp[core, y, at, :].astype(F32) + crs[y, at, :].astype(F32)
            for k in range(3):
                s = s + fyr[k, at, :].astype(F32)
            out[p] = s

        each(8, finish)

    pl.run_scoped(
        backward_sweep,
        pltpu.VMEM((K, LOW, TALL), BF),
        pltpu.VMEM((NOFF, TALL, LOW), BF),
        pltpu.VMEM((30, TALL, R), F32),
    )


def on_device(right_sides, lower_inv, lower_off, upper_inv, upper_off, present):
    shares = jnp.pad(right_sides, ((0, 1), (0, 0), (0, 0))).reshape(16, 2 * SMALL, R)
    shares = jnp.pad(shares, ((0, 0), (0, PAIR - 2 * SMALL), (0, 0))).reshape(2, 8 * PAIR, R)
    put, take = placing()
    vmem = pl.BlockSpec(memory_space=pltpu.VMEM)
    hbm = pl.BlockSpec(memory_space=pl.ANY)
    out = pl.pallas_call(
        kernel,
        out_shape=jax.ShapeDtypeStruct((16, PAIR, R), F32),
        in_specs=[vmem, vmem, vmem, pl.BlockSpec(memory_space=pltpu.SMEM), hbm, hbm, hbm, hbm],
        out_specs=vmem,
        scratch_shapes=[
            pltpu.VMEM((2, 4, 1216, H), BF),
            pltpu.VMEM((2, 3, 1216, H), BF),
            pltpu.VMEM((2, 1216, H), BF),
            pltpu.VMEM((2, 3, 1216, H), BF),
            pltpu.VMEM((2, 4, 1216, H), BF),
            pltpu.VMEM((2, FWROWS, H), F32),
            pltpu.VMEM((2, 1216, H), F32),
            pltpu.VMEM((2, 8 * PITCH, H), BF),
            pltpu.VMEM((8 * PITCH, H), BF),
            pltpu.VMEM((8 * PITCH, H), F32),
            pltpu.VMEM((8 * PITCH, H), BF),
            pltpu.VMEM((2, 3, 8 * PITCH, H), BF),
            pltpu.VMEM((2, 16 * PITCH, H), BF),
            pltpu.VMEM((2, 15 * PITCH, H), BF),
            pltpu.VMEM((2, 4, 8 * PAIR, R), BF),
            pltpu.VMEM((2, 4, 8 * PAIR, R), BF),
            pltpu.VMEM((2, 4, 8 * PAIR, R), BF),
            pltpu.VMEM((4, 8 * PAIR, R), BF),
            pltpu.VMEM((4, 8 * PAIR, R), BF),
            pltpu.VMEM((3, 8 * PAIR, R), BF),
            pltpu.SemaphoreType.DMA((NSEM,)),
            pltpu.SemaphoreType.DMA((NSEM,)),
            pltpu.SemaphoreType.DMA((9,)),
        ],
        compiler_params=pltpu.CompilerParams(
            collective_id=0, has_side_effects=True, vmem_limit_bytes=60 * 1024 * 1024
        ),
    )(
        shares,
        jnp.asarray(put, BF),
        jnp.asarray(take, BF),
        present,
        lower_inv,
        lower_off,
        upper_inv,
        upper_off,
    )
    return out[:, : 2 * SMALL].reshape(32, SMALL, R)[:K]


def solution(mesh):
    placed = (
        P(None, ("row", "col"), None),
        P(None, "col", "row"),
        P(None, "row", "col"),
        P(None, "row", "col"),
        P(None, "col", "row"),
        P(),
    )
    return jax.shard_map(
        on_device,
        mesh=mesh,
        in_specs=placed,
        out_specs=P(None, ("row", "col"), None),
        check_vma=False,
    )
```

```python
import jax
import jax.numpy as jnp
from jax import lax
from jax.experimental import pallas as pl
from jax.experimental.pallas import tpu as pltpu
from jax.sharding import PartitionSpec as P

LEVELS = 5
K = 31
NOFF = 98
R = 256
H = 128
TALL = 304
LOW = 152
PITCH = 160
SMALL = 19
SHARES = 304
MEMBERS = [16, 8, 4, 2, 1]
NODE = [0, 16, 24, 28, 30]
SLOT = [0, 64, 88, 96, 98]
PIECE = {8: 608, 4: 304, 2: 160, 1: 80}
FWROW = [0, 608, 912, 1072, 1152]
FWROWS = 1232
MESH = pl.DeviceIdType.MESH
BF = jnp.bfloat16
F32 = jnp.float32

RS, EX, AG, CR, CG, YX, HALF = 0, 6, 12, 18, 19, 20, 26
IY, IC, FC, FY = 52, 64, 68, 70
NSEM = 76


def dot(a, b):
    return jnp.dot(a, b, preferred_element_type=F32)


def dot_first(a, b):
    return lax.dot_general(a, b, (((0,), (0,)), ((), ())), preferred_element_type=F32)


def kernel(
    rs, present, linv, loff, uinv, uoff, out,
    pb, rb, es, eb, xb, fw, tot, cb, crb, ct, ys, yb, lowb, rg, ag0, ag1, wide, shown, sp, crs, fys, fyr,
    ssem, rsem, wsem,
):
    row, col = lax.axis_index("row"), lax.axis_index("col")
    z, x = row // 4, row % 4
    y, core = col // 2, col % 2
    sibling = (row, y * 2 + 1 - core)
    along = (z, x)

    def zpeer(d):
        return (((z + d) % 4) * 4 + x, col)

    def xpeer(d):
        return (z * 4 + (x + d) % 4, col)

    def ypeer(d):
        return (row, ((y + d) % 4) * 2 + core)

    first_peer = (zpeer, xpeer)
    second_peer = (xpeer, zpeer)

    for h in (0, 1):
        part = slice(h * H, (h + 1) * H)
        ag0[h, y, core] = rs[:, 0:16, part]
        ag1[h, y, core] = jnp.concatenate(
            [rs[:, 16:31, part], jnp.zeros((SMALL, 1, H), BF)], axis=1
        )

    barrier = pltpu.get_barrier_semaphore()
    for d in (1, 2, 3):
        for peer in (zpeer, xpeer, ypeer):
            pl.semaphore_signal(barrier, inc=1, device_id=peer(d), device_id_type=MESH)
    pl.semaphore_signal(barrier, inc=1, device_id=sibling, device_id_type=MESH)
    pl.semaphore_wait(barrier, 10)

    def send(src, dst, sem, to):
        c = pltpu.make_async_remote_copy(
            src, dst, ssem.at[sem], rsem.at[sem], device_id=to, device_id_type=MESH
        )
        c.start()
        return c

    def wait(copies):
        for c in copies:
            c.wait()

    def chunks(rows, chunk, body):
        if rows == chunk:
            body(pl.ds(0, chunk), 0)
        else:

            def step(i, _):
                at = pl.multiple_of(i * chunk, 16)
                body(pl.ds(at, chunk), at)
                return 0

            lax.fori_loop(0, rows // chunk, step, 0)

    def each(n, body):
        if n <= 2:
            for i in range(n):
                body(i)
        else:

            def step(i, _):
                body(i)
                return 0

            lax.fori_loop(0, n, step, 0)

    def tall_get(ref, m, j):
        if m >= 4:
            per = m // 4
            q, at = j // per, (j % per) * TALL
            if not isinstance(at, int):
                at = pl.multiple_of(at, 16)
            halves = [ref[h, q, pl.ds(at, TALL), :] for h in (0, 1)]
        elif m == 2:
            halves = [
                jnp.concatenate([ref[h, 2 * j, 0:160, :], ref[h, 2 * j + 1, 0:144, :]], axis=0)
                for h in (0, 1)
            ]
        else:
            halves = [
                jnp.concatenate(
                    [ref[h, q, 0:80, :] for q in range(3)] + [ref[h, 3, 0:64, :]], axis=0
                )
                for h in (0, 1)
            ]
        return jnp.concatenate(halves, axis=1)

    def tall_put(ref, m, j, value):
        value = value.astype(BF)
        for h in (0, 1):
            v = value[:, h * H : (h + 1) * H]
            if m >= 4:
                per = m // 4
                q, at = j // per, (j % per) * TALL
                if not isinstance(at, int):
                    at = pl.multiple_of(at, 16)
                ref[h, q, pl.ds(at, TALL), :] = v
            elif m == 2:
                ref[h, 2 * j, 0:160, :] = v[0:160]
                ref[h, 2 * j + 1, 0:144, :] = v[160:304]
            else:
                for q in range(3):
                    ref[h, q, 0:80, :] = v[80 * q : 80 * q + 80]
                ref[h, 3, 0:64, :] = v[240:304]

    def low_rows(j):
        at = j * PITCH
        return pl.ds(at if isinstance(at, int) else pl.multiple_of(at, 16), LOW)

    def low_get(ref, j):
        return jnp.concatenate([ref[h, low_rows(j), :] for h in (0, 1)], axis=1)

    def low_put(ref, j, value):
        value = value.astype(BF)
        for h in (0, 1):
            ref[h, low_rows(j), :] = value[:, h * H : (h + 1) * H]

    def row_reduce(t, m, level, forward):
        rows, base, sem = PIECE[m], FWROW[level], HALF * t
        chunk = min(rows, TALL)
        first = [
            [
                send(
                    pb.at[t, h, (along[h] + d) % 4, pl.ds(0, rows)],
                    rb.at[t, h, d - 1, pl.ds(0, rows)],
                    sem + RS + h * 3 + d - 1,
                    first_peer[h](d),
                )
                for d in (2, 1, 3)
            ]
            for h in (0, 1)
        ]
        yield
        second = []
        for h in (0, 1):
            wait(first[h])

            def add(at, _, h=h):
                s = pb[t, h, along[h], at, :].astype(F32)
                for k in range(3):
                    s = s + rb[t, h, k, at, :].astype(F32)
                tot[t, h, at, :] = s
                es[t, h, at, :] = s.astype(BF)

            chunks(rows, chunk, add)
            second.append(
                [
                    send(
                        es.at[t, h, pl.ds(0, rows)],
                        eb.at[t, h, d - 1, pl.ds(0, rows)],
                        sem + EX + h * 3 + d - 1,
                        second_peer[h](d),
                    )
                    for d in (2, 1, 3)
                ]
            )
        yield
        third = []
        for h in (0, 1):
            wait(second[h])

            def last(at, start, h=h):
                s = tot[t, h, at, :]
                for k in range(3):
                    s = s + eb[t, h, k, at, :].astype(F32)
                kept = pl.ds(
                    base + start if isinstance(start, int) else pl.multiple_of(base + start, 16),
                    chunk,
                )
                if forward:
                    fw[t, h, kept, :] = s
                else:
                    s = fw[t, h, kept, :] - s
                xb[t, h, along[h], at, :] = s.astype(BF)

            chunks(rows, chunk, last)
            mine = xb.at[t, h, along[h], pl.ds(0, rows)]
            third.append(
                [send(mine, mine, sem + AG + h * 3 + d - 1, first_peer[h](d)) for d in (2, 1, 3)]
            )
        yield
        for h in (0, 1):
            wait(third[h])

    turns = [0, 0]

    def col_reduce(t, m, base=None, aside=None):
        rows, sem, turn = m * PITCH, HALF * t, turns[t]
        turns[t] = 1 - turn
        copies = [
            send(cb.at[t, 1 - core, pl.ds(0, rows)], crb.at[t, pl.ds(0, rows)], sem + CR, sibling)
        ]
        yield
        wait(copies)

        def add(at, _):
            s = cb[t, core, at, :].astype(F32) + crb[t, at, :].astype(F32)
            ct[t, at, :] = s
            ys[t, at, :] = s.astype(BF)

        chunks(rows, PITCH, add)
        copies = [
            send(
                ys.at[t, pl.ds(0, rows)],
                yb.at[t, turn, d - 1, pl.ds(0, rows)],
                sem + YX + turn * 3 + d - 1,
                ypeer(d),
            )
            for d in (2, 1, 3)
        ]
        if aside is not None:
            aside()
        yield
        wait(copies)

        def last(at, start):
            s = ct[t, at, :]
            for k in range(3):
                s = s + yb[t, turn, k, at, :].astype(F32)
            if base is not None:
                first = base + start
                if not isinstance(start, int):
                    first = pl.multiple_of(first, 16)
                s = rg[core, pl.ds(first, PITCH), :].astype(F32) - s
            lowb[t, core, at, :] = s.astype(BF)

        chunks(rows, PITCH, last)
        mine = lowb.at[t, core, pl.ds(0, rows)]
        copies = [send(mine, mine, sem + CG, sibling)]
        yield
        wait(copies)

    def gather_y(part, buf):
        return [
            [
                send(
                    buf.at[h, y, core],
                    buf.at[h, y, core],
                    IY + part * 6 + h * 3 + d - 1,
                    ypeer(d),
                )
                for d in (2, 1, 3)
            ]
            for h in (0, 1)
        ]

    def gather_core(part, buf, copies):
        more = []
        for h in (0, 1):
            wait(copies[h])
            mine = buf.at[h, :, core]
            more.append(send(mine, mine, IC + part * 2 + h, sibling))
        return more

    def unpack(copies, buf, members, place):
        for h in (0, 1):
            wait([copies[h]])
            for c in range(8):
                v = buf[h, c // 2, c % 2].astype(F32).reshape(SHARES, H)
                wide[h, pl.ds(c * SHARES, SHARES), :] = v
            for j in range(members):
                v = wide[h, pl.ds(j, LOW, stride=16), :]
                place(h, j, v.astype(BF))

    def col_steps(*args):
        for _ in col_reduce(*args):
            yield 1

    def row_steps(*args):
        for _ in row_reduce(*args):
            yield 1

    def run(halves):
        halves = list(halves)
        while halves:
            for g in list(halves):
                if next(g, 0) == 0:
                    halves.remove(g)

    def fetch(src, dst, first, n, sem):
        c = pltpu.make_async_copy(src.at[pl.ds(first, n)], dst.at[pl.ds(first, n)], wsem.at[sem])
        c.start()
        return c

    def forward_sweep(li, lo, waiting):
        inv_copy, off_copy = [], []
        ic0 = gather_y(0, ag0)
        ic1 = gather_y(1, ag1)
        for level in range(LEVELS):
            inv_copy.append(fetch(linv, li, NODE[level], MEMBERS[level], level))
            if level < 4:
                off_copy.append(
                    fetch(loff, lo, SLOT[level], SLOT[level + 1] - SLOT[level], 5 + level)
                )
        waiting[...] = jnp.zeros_like(waiting)

        def leaves(h, j, v):
            lowb[j // 8, h, low_rows(j % 8), :] = v

        def others(h, j, v):
            rg[h, low_rows(j), :] = v

        def solve(t, m, level):
            first = NODE[level] + t * m

            def one(j):
                tall_put(pb.at[t], m, j, dot_first(li[first + j], low_get(lowb.at[t], j)))

            each(m, one)

        def product(t, m, level, j, a):
            above = LEVELS - 1 - level
            slot = SLOT[level] + (t * m + j) * above + a - 1
            scale = present[slot].astype(F32)
            return scale * dot(lo[slot], tall_get(xb.at[t], m, j))

        def half(t):
            for level in range(4):
                m = MEMBERS[level] // 2
                above = LEVELS - 1 - level
                if t == 0:
                    inv_copy[level].wait()
                solve(t, m, level)
                for _ in row_reduce(t, m, level, True):
                    yield 1
                if t == 0:
                    off_copy[level].wait()
                if level == 3:
                    break
                to = NODE[level + 1] - 16 + t * (m // 2)

                def near(k, level=level, m=m, to=to):
                    value = product(t, m, level, 2 * k, 1) + product(t, m, level, 2 * k + 1, 1)
                    if level > 0:
                        value = value + waiting[to + k]
                    low_put(cb.at[t], k, value)

                each(m // 2, near)

                def far(level=level, m=m, above=above):
                    def one(j):
                        for a in range(2, above + 1):
                            k = NODE[level + a] - 16 + (t * m + j) // 2**a
                            waiting[k] = waiting[k] + product(t, m, level, j, a)

                    each(m, one)

                for _ in col_reduce(t, m // 2, to * PITCH, far):
                    yield 1

        unpack(gather_core(0, ag0, ic0), ag0, 16, leaves)
        halves = [half(0), half(1)]
        for g in halves:
            next(g)
        unpack(gather_core(1, ag1, ic1), ag1, 15, others)
        run(halves)
        low_put(cb.at[0], 0, waiting[14] + product(0, 1, 3, 0, 1) + product(1, 1, 3, 0, 1))
        run([col_steps(0, 1, 14 * PITCH)])
        inv_copy[4].wait()
        solve(0, 1, 4)
        run([row_steps(0, 1, 4, True)])

    pl.run_scoped(
        forward_sweep,
        pltpu.VMEM((K, LOW, TALL), BF),
        pltpu.VMEM((NOFF, LOW, TALL), BF),
        pltpu.VMEM((15, LOW, R), F32),
    )

    def backward_sweep(ui, uo, upward):
        spot = lax.broadcasted_iota(jnp.int32, (24, LOW), 1)
        at_row = lax.broadcasted_iota(jnp.int32, (24, LOW), 0) + col * SMALL
        own = jnp.where(spot == at_row, 1.0, 0.0).astype(BF)
        inv_copy, off_copy = {}, {}
        for level in reversed(range(LEVELS)):
            if level < 4:
                off_copy[level] = fetch(
                    uoff, uo, SLOT[level], SLOT[level + 1] - SLOT[level], 5 + level
                )
            inv_copy[level] = fetch(uinv, ui, NODE[level], MEMBERS[level], level)

        def solve(t, m, level):
            first = NODE[level] + t * m

            def one(j):
                low_put(cb.at[t], j, dot(ui[first + j], tall_get(xb.at[t], m, j)))

            each(m, one)

        def product(t, level, under, j, k):
            slot = SLOT[under] + j * (LEVELS - 1 - under) + level - under - 1
            scale = present[slot].astype(F32)
            return scale * dot_first(uo[slot], low_get(lowb.at[t], k))

        def show(t, m, level):
            for j in range(m):
                v = dot(own, low_get(lowb.at[t], j))[:SMALL]
                for h in (0, 1):
                    shown[h, pl.ds(NODE[level] - 16 + t * m + j, SMALL, stride=16), :] = v[
                        :, h * H : (h + 1) * H
                    ]

        inv_copy[4].wait()
        solve(0, 1, 4)
        run([col_steps(0, 1)])
        off_copy[3].wait()
        for t in (0, 1):
            tall_put(pb.at[t], 1, 0, product(0, 4, 3, t, 0))

        def half(t):
            for _ in row_reduce(t, 1, 3, False):
                yield 1
            for level in (3, 2, 1):
                m = MEMBERS[level] // 2
                if t == 0:
                    inv_copy[level].wait()
                solve(t, m, level)
                for _ in col_reduce(t, m):
                    yield 1

                def near(i, level=level, m=m):
                    j = t * 2 * m + i
                    value = product(t, level, level - 1, j, i // 2)
                    tall_put(pb.at[t], 2 * m, i, value + upward[NODE[level - 1] + j])

                each(2 * m, near)
                steps = row_reduce(t, 2 * m, level - 1, False)
                next(steps)
                for under in range(level - 2, -1, -1):

                    def far(i, level=level, m=m, under=under):
                        j = t * (MEMBERS[under] // 2) + i
                        value = product(t, level, under, j, i // 2 ** (level - under))
                        upward[NODE[under] + j] = value + upward[NODE[under] + j]

                    each(MEMBERS[under] // 2, far)
                show(t, m, level)
                yield 1
                for _ in steps:
                    yield 1

        halves = [half(0), half(1)]
        for g in halves:
            next(g)
        for under in (2, 1, 0):
            off_copy[under].wait()

            def root_far(j, under=under):
                upward[NODE[under] + j] = product(0, 4, under, j, 0)

            each(MEMBERS[under], root_far)
        show(0, 1, 4)
        run(halves)

        inv_copy[0].wait()
        for j in range(16):
            v = dot(ui[j], tall_get(xb.at[j // 8], 8, j % 8))
            for h in (0, 1):
                wide[h, pl.ds(j, LOW, stride=16), :] = v[:, h * H : (h + 1) * H]
        first = []
        for h in (0, 1):
            for c in range(8):
                sp[h, c // 2, c % 2] = wide[h, pl.ds(c * SHARES, SHARES), :].astype(BF)
            first.append(send(sp.at[h, :, 1 - core], crs.at[h], FC + h, sibling))
        second = []
        for h in (0, 1):
            wait([first[h]])
            copies = []
            for d in (2, 1, 3):
                to = (y + d) % 4
                fys[h, to] = (sp[h, to, core].astype(F32) + crs[h, to].astype(F32)).astype(BF)
                copies.append(send(fys.at[h, to], fyr.at[h, d - 1], FY + h * 3 + d - 1, ypeer(d)))
            second.append(copies)

        def move(i):
            at = pl.ds(pl.multiple_of(i * 16, 16), 16)
            to = pl.ds(pl.multiple_of(i * 32 + 16, 16), 16)
            for h in (0, 1):
                out[to, h * H : (h + 1) * H] = shown[h, at, :]

        each(SMALL, move)
        for h in (0, 1):
            wait(second[h])

            def finish(i, h=h):
                at = pl.ds(pl.multiple_of(i * 16, 16), 16)
                s = sp[h, y, core, at, :].astype(F32) + crs[h, y, at, :].astype(F32)
                for k in range(3):
                    s = s + fyr[h, k, at, :].astype(F32)
                out[pl.ds(pl.multiple_of(i * 32, 32), 16), h * H : (h + 1) * H] = s

            each(SMALL, finish)

    pl.run_scoped(
        backward_sweep,
        pltpu.VMEM((K, LOW, TALL), BF),
        pltpu.VMEM((NOFF, LOW, TALL), BF),
        pltpu.VMEM((30, TALL, R), F32),
    )


def on_device(right_sides, lower_inv, lower_off, upper_inv, upper_off, present):
    vmem = pl.BlockSpec(memory_space=pltpu.VMEM)
    hbm = pl.BlockSpec(memory_space=pl.ANY)
    out = pl.pallas_call(
        kernel,
        out_shape=jax.ShapeDtypeStruct((32 * SMALL, R), F32),
        in_specs=[vmem, pl.BlockSpec(memory_space=pltpu.SMEM), hbm, hbm, hbm, hbm],
        out_specs=vmem,
        scratch_shapes=[
            pltpu.VMEM((2, 2, 4, 608, H), BF),
            pltpu.VMEM((2, 2, 3, 608, H), BF),
            pltpu.VMEM((2, 2, 608, H), BF),
            pltpu.VMEM((2, 2, 3, 608, H), BF),
            pltpu.VMEM((2, 2, 4, 608, H), BF),
            pltpu.VMEM((2, 2, FWROWS, H), F32),
            pltpu.VMEM((2, 2, 608, H), F32),
            pltpu.VMEM((2, 2, 4 * PITCH, H), BF),
            pltpu.VMEM((2, 4 * PITCH, H), BF),
            pltpu.VMEM((2, 4 * PITCH, H), F32),
            pltpu.VMEM((2, 4 * PITCH, H), BF),
            pltpu.VMEM((2, 2, 3, 4 * PITCH, H), BF),
            pltpu.VMEM((2, 2, 8 * PITCH, H), BF),
            pltpu.VMEM((2, 15 * PITCH, H), BF),
            pltpu.VMEM((2, 4, 2, SMALL, 16, H), BF),
            pltpu.VMEM((2, 4, 2, SMALL, 16, H), BF),
            pltpu.VMEM((2, 8 * SHARES, H), F32),
            pltpu.VMEM((2, SHARES, H), F32),
            pltpu.VMEM((2, 4, 2, SHARES, H), BF),
            pltpu.VMEM((2, 4, SHARES, H), BF),
            pltpu.VMEM((2, 4, SHARES, H), BF),
            pltpu.VMEM((2, 3, SHARES, H), BF),
            pltpu.SemaphoreType.DMA((NSEM,)),
            pltpu.SemaphoreType.DMA((NSEM,)),
            pltpu.SemaphoreType.DMA((9,)),
        ],
        compiler_params=pltpu.CompilerParams(
            collective_id=0, has_side_effects=True, vmem_limit_bytes=60 * 1024 * 1024
        ),
    )(
        jnp.swapaxes(right_sides, 0, 1),
        present,
        jnp.swapaxes(lower_inv, 1, 2),
        lower_off,
        upper_inv,
        jnp.swapaxes(upper_off, 1, 2),
    )
    return jnp.swapaxes(out.reshape(SMALL, 32, R)[:, :K], 0, 1)


def solution(mesh):
    placed = (
        P(None, ("row", "col"), None),
        P(None, "col", "row"),
        P(None, "row", "col"),
        P(None, "row", "col"),
        P(None, "col", "row"),
        P(),
    )
    return jax.shard_map(
        on_device,
        mesh=mesh,
        in_specs=placed,
        out_specs=P(None, ("row", "col"), None),
        check_vma=False,
    )
```

```python
import jax
import jax.numpy as jnp
from jax import lax
from jax.experimental import pallas as pl
from jax.experimental.pallas import tpu as pltpu
from jax.sharding import PartitionSpec as P

LEVELS = 5
K = 31
NOFF = 98
R = 256
H = 128
TALL = 304
LOW = 152
PITCH = 160
SMALL = 19
SHARES = 304
MEMBERS = [16, 8, 4, 2, 1]
NODE = [0, 16, 24, 28, 30]
SLOT = [0, 64, 88, 96, 98]
PIECE = {8: 608, 4: 304, 2: 160, 1: 80}
FWROW = [0, 608, 912, 1072, 1152]
FWROWS = 1232
MESH = pl.DeviceIdType.MESH
BF = jnp.bfloat16
F32 = jnp.float32

RS, EX, AG, CR, CG, YX, HALF = 0, 6, 12, 18, 19, 20, 26
IY, IC, FC, FY = 52, 64, 68, 70
NSEM = 76


def dot(a, b):
    return jnp.dot(a, b, preferred_element_type=F32)


def dot_first(a, b):
    return lax.dot_general(a, b, (((0,), (0,)), ((), ())), preferred_element_type=F32)


def kernel(
    rs, present, linv, loff, uinv, uoff, out,
    pb, rb, es, eb, xb, fw, tot, cb, crb, ct, ys, yb, lowb, topb, rg, ag0, ag1, wide, shown, sp, crs, fys, fyr,
    ssem, rsem, wsem,
):
    row, col = lax.axis_index("row"), lax.axis_index("col")
    z, x = row // 4, row % 4
    y, core = col // 2, col % 2
    sibling = (row, y * 2 + 1 - core)
    along = (z, x)

    def zpeer(d):
        return (((z + d) % 4) * 4 + x, col)

    def xpeer(d):
        return (z * 4 + (x + d) % 4, col)

    def ypeer(d):
        return (row, ((y + d) % 4) * 2 + core)

    first_peer = (zpeer, xpeer)
    second_peer = (xpeer, zpeer)

    for h in (0, 1):
        part = slice(h * H, (h + 1) * H)
        ag0[h, y, core] = rs[:, 0:16, part]
        ag1[h, y, core] = jnp.concatenate(
            [rs[:, 16:31, part], jnp.zeros((SMALL, 1, H), BF)], axis=1
        )

    barrier = pltpu.get_barrier_semaphore()
    for d in (1, 2, 3):
        for peer in (zpeer, xpeer, ypeer):
            pl.semaphore_signal(barrier, inc=1, device_id=peer(d), device_id_type=MESH)
    pl.semaphore_signal(barrier, inc=1, device_id=sibling, device_id_type=MESH)
    pl.semaphore_wait(barrier, 10)

    def send(src, dst, sem, to):
        c = pltpu.make_async_remote_copy(
            src, dst, ssem.at[sem], rsem.at[sem], device_id=to, device_id_type=MESH
        )
        c.start()
        return c

    def wait(copies):
        for c in copies:
            c.wait()

    def chunks(rows, chunk, body):
        if rows == chunk:
            body(pl.ds(0, chunk), 0)
        else:

            def step(i, _):
                at = pl.multiple_of(i * chunk, 16)
                body(pl.ds(at, chunk), at)
                return 0

            lax.fori_loop(0, rows // chunk, step, 0)

    def each(n, body):
        if n <= 2:
            for i in range(n):
                body(i)
        else:

            def step(i, _):
                body(i)
                return 0

            lax.fori_loop(0, n, step, 0, unroll=2 if n % 2 == 0 else 1)

    def tall_get(ref, m, j):
        if m >= 4:
            per = m // 4
            q, at = j // per, (j % per) * TALL
            if not isinstance(at, int):
                at = pl.multiple_of(at, 16)
            halves = [ref[h, q, pl.ds(at, TALL), :] for h in (0, 1)]
        elif m == 2:
            halves = [
                jnp.concatenate([ref[h, 2 * j, 0:160, :], ref[h, 2 * j + 1, 0:144, :]], axis=0)
                for h in (0, 1)
            ]
        else:
            halves = [
                jnp.concatenate(
                    [ref[h, q, 0:80, :] for q in range(3)] + [ref[h, 3, 0:64, :]], axis=0
                )
                for h in (0, 1)
            ]
        return jnp.concatenate(halves, axis=1)

    def tall_put(ref, m, j, value):
        value = value.astype(BF)
        for h in (0, 1):
            v = value[:, h * H : (h + 1) * H]
            if m >= 4:
                per = m // 4
                q, at = j // per, (j % per) * TALL
                if not isinstance(at, int):
                    at = pl.multiple_of(at, 16)
                ref[h, q, pl.ds(at, TALL), :] = v
            elif m == 2:
                ref[h, 2 * j, 0:160, :] = v[0:160]
                ref[h, 2 * j + 1, 0:144, :] = v[160:304]
            else:
                for q in range(3):
                    ref[h, q, 0:80, :] = v[80 * q : 80 * q + 80]
                ref[h, 3, 0:64, :] = v[240:304]

    def low_rows(j):
        at = j * PITCH
        return pl.ds(at if isinstance(at, int) else pl.multiple_of(at, 16), LOW)

    def low_get(ref, j):
        return jnp.concatenate([ref[h, low_rows(j), :] for h in (0, 1)], axis=1)

    def low_put(ref, j, value):
        value = value.astype(BF)
        for h in (0, 1):
            ref[h, low_rows(j), :] = value[:, h * H : (h + 1) * H]

    def row_reduce(t, m, level, forward):
        rows, base, sem = PIECE[m], FWROW[level], HALF * t
        chunk = min(rows, TALL)
        first = [
            [
                send(
                    pb.at[t, h, (along[h] + d) % 4, pl.ds(0, rows)],
                    rb.at[t, h, d - 1, pl.ds(0, rows)],
                    sem + RS + h * 3 + d - 1,
                    first_peer[h](d),
                )
                for d in (2, 1, 3)
            ]
            for h in (0, 1)
        ]
        yield
        second = []
        for h in (0, 1):
            wait(first[h])

            def add(at, _, h=h):
                s = pb[t, h, along[h], at, :].astype(F32)
                for k in range(3):
                    s = s + rb[t, h, k, at, :].astype(F32)
                tot[t, h, at, :] = s
                es[t, h, at, :] = s.astype(BF)

            chunks(rows, chunk, add)
            second.append(
                [
                    send(
                        es.at[t, h, pl.ds(0, rows)],
                        eb.at[t, h, d - 1, pl.ds(0, rows)],
                        sem + EX + h * 3 + d - 1,
                        second_peer[h](d),
                    )
                    for d in (2, 1, 3)
                ]
            )
        yield
        third = []
        for h in (0, 1):
            wait(second[h])

            def last(at, start, h=h):
                s = tot[t, h, at, :]
                for k in range(3):
                    s = s + eb[t, h, k, at, :].astype(F32)
                kept = pl.ds(
                    base + start if isinstance(start, int) else pl.multiple_of(base + start, 16),
                    chunk,
                )
                if forward:
                    fw[t, h, kept, :] = s
                else:
                    s = fw[t, h, kept, :] - s
                xb[t, h, along[h], at, :] = s.astype(BF)

            chunks(rows, chunk, last)
            mine = xb.at[t, h, along[h], pl.ds(0, rows)]
            third.append(
                [send(mine, mine, sem + AG + h * 3 + d - 1, first_peer[h](d)) for d in (2, 1, 3)]
            )
        yield
        for h in (0, 1):
            wait(third[h])

    turns = [0, 0]

    def col_reduce(t, m, base=None, aside=None):
        rows, sem, turn = m * PITCH, HALF * t, turns[t]
        turns[t] = 1 - turn
        copies = [
            send(cb.at[t, 1 - core, pl.ds(0, rows)], crb.at[t, pl.ds(0, rows)], sem + CR, sibling)
        ]
        yield
        wait(copies)

        def add(at, _):
            s = cb[t, core, at, :].astype(F32) + crb[t, at, :].astype(F32)
            ct[t, at, :] = s
            ys[t, at, :] = s.astype(BF)

        chunks(rows, PITCH, add)
        copies = [
            send(
                ys.at[t, pl.ds(0, rows)],
                yb.at[t, turn, d - 1, pl.ds(0, rows)],
                sem + YX + turn * 3 + d - 1,
                ypeer(d),
            )
            for d in (2, 1, 3)
        ]
        if aside is not None:
            yield
            aside()
        yield
        wait(copies)

        def last(at, start):
            s = ct[t, at, :]
            for k in range(3):
                s = s + yb[t, turn, k, at, :].astype(F32)
            if base is not None:
                first = base + start
                if not isinstance(start, int):
                    first = pl.multiple_of(first, 16)
                s = rg[core, pl.ds(first, PITCH), :].astype(F32) - s
            lowb[t, core, at, :] = s.astype(BF)

        chunks(rows, PITCH, last)
        mine = lowb.at[t, core, pl.ds(0, rows)]
        copies = [send(mine, mine, sem + CG, sibling)]
        yield
        wait(copies)

    def gather_y(part, buf):
        return [
            [
                send(
                    buf.at[h, y, core],
                    buf.at[h, y, core],
                    IY + part * 6 + h * 3 + d - 1,
                    ypeer(d),
                )
                for d in (2, 1, 3)
            ]
            for h in (0, 1)
        ]

    def gather_core(part, buf, copies):
        more = []
        for h in (0, 1):
            wait(copies[h])
            mine = buf.at[h, :, core]
            more.append(send(mine, mine, IC + part * 2 + h, sibling))
        return more

    def unpack(copies, buf, members, place):
        for h in (0, 1):
            wait([copies[h]])
            for c in range(8):
                v = buf[h, c // 2, c % 2].astype(F32).reshape(SHARES, H)
                wide[h, pl.ds(c * SHARES, SHARES), :] = v
            for j in range(members):
                v = wide[h, pl.ds(j, LOW, stride=16), :]
                place(h, j, v.astype(BF))

    def col_steps(*args):
        for _ in col_reduce(*args):
            yield 1

    def row_steps(*args):
        for _ in row_reduce(*args):
            yield 1

    def run(halves):
        halves = list(halves)
        while halves:
            for g in list(halves):
                if next(g, 0) == 0:
                    halves.remove(g)

    def fetch(src, dst, first, n, sem):
        c = pltpu.make_async_copy(src.at[pl.ds(first, n)], dst.at[pl.ds(first, n)], wsem.at[sem])
        c.start()
        return c

    def forward_sweep(li, lo, waiting):
        inv_copy, off_copy = [], []
        ic0 = gather_y(0, ag0)
        ic1 = gather_y(1, ag1)
        for level in range(LEVELS):
            inv_copy.append(fetch(linv, li, NODE[level], MEMBERS[level], level))
            if level < 4:
                off_copy.append(
                    fetch(loff, lo, SLOT[level], SLOT[level + 1] - SLOT[level], 5 + level)
                )
        waiting[...] = jnp.zeros_like(waiting)

        def leaves(h, j, v):
            lowb[j // 8, h, low_rows(j % 8), :] = v

        def others(h, j, v):
            rg[h, low_rows(j), :] = v

        def solve(t, m, level):
            first = NODE[level] + t * m

            def one(j):
                tall_put(pb.at[t], m, j, dot_first(li[first + j], low_get(lowb.at[t], j)))

            each(m, one)

        def product(t, m, level, j, a):
            above = LEVELS - 1 - level
            slot = SLOT[level] + (t * m + j) * above + a - 1
            scale = present[slot].astype(F32)
            return scale * dot(lo[slot], tall_get(xb.at[t], m, j))

        def half(t):
            for level in range(4):
                m = MEMBERS[level] // 2
                above = LEVELS - 1 - level
                if t == 0:
                    inv_copy[level].wait()
                solve(t, m, level)
                for _ in row_reduce(t, m, level, True):
                    yield 1
                if t == 0:
                    off_copy[level].wait()
                if level == 3:
                    break
                to = NODE[level + 1] - 16 + t * (m // 2)

                def near(k, level=level, m=m, to=to):
                    value = product(t, m, level, 2 * k, 1) + product(t, m, level, 2 * k + 1, 1)
                    if level > 0:
                        value = value + waiting[to + k]
                    low_put(cb.at[t], k, value)

                each(m // 2, near)

                def far(level=level, m=m, above=above):
                    def one(j):
                        for a in range(2, above + 1):
                            k = NODE[level + a] - 16 + (t * m + j) // 2**a
                            waiting[k] = waiting[k] + product(t, m, level, j, a)

                    each(m, one)

                for _ in col_reduce(t, m // 2, to * PITCH, far):
                    yield 1

        unpack(gather_core(0, ag0, ic0), ag0, 16, leaves)
        halves = [half(0), half(1)]
        for g in halves:
            next(g)
        unpack(gather_core(1, ag1, ic1), ag1, 15, others)
        run(halves)
        low_put(cb.at[0], 0, waiting[14] + product(0, 1, 3, 0, 1) + product(1, 1, 3, 0, 1))
        run([col_steps(0, 1, 14 * PITCH)])
        inv_copy[4].wait()
        solve(0, 1, 4)
        run([row_steps(0, 1, 4, True)])

    pl.run_scoped(
        forward_sweep,
        pltpu.VMEM((K, LOW, TALL), BF),
        pltpu.VMEM((NOFF, LOW, TALL), BF),
        pltpu.VMEM((15, LOW, R), F32),
    )

    def backward_sweep(ui, uo, upward):
        spot = lax.broadcasted_iota(jnp.int32, (24, LOW), 1)
        at_row = lax.broadcasted_iota(jnp.int32, (24, LOW), 0) + col * SMALL
        own = jnp.where(spot == at_row, 1.0, 0.0).astype(BF)
        inv_copy, off_copy = {}, {}
        for level in reversed(range(LEVELS)):
            if level < 4:
                off_copy[level] = fetch(
                    uoff, uo, SLOT[level], SLOT[level + 1] - SLOT[level], 5 + level
                )
            inv_copy[level] = fetch(uinv, ui, NODE[level], MEMBERS[level], level)

        def solve(t, m, level):
            first = NODE[level] + t * m

            def one(j):
                low_put(cb.at[t], j, dot(ui[first + j], tall_get(xb.at[t], m, j)))

            each(m, one)

        def product(t, level, under, j, k):
            slot = SLOT[under] + j * (LEVELS - 1 - under) + level - under - 1
            scale = present[slot].astype(F32)
            return scale * dot_first(uo[slot], low_get(lowb.at[t], k))

        def show(t, m, level):
            for j in range(m):
                v = dot(own, low_get(lowb.at[t], j))[:SMALL]
                for h in (0, 1):
                    shown[h, pl.ds(NODE[level] - 16 + t * m + j, SMALL, stride=16), :] = v[
                        :, h * H : (h + 1) * H
                    ]

        inv_copy[4].wait()
        solve(0, 1, 4)
        run([col_steps(0, 1)])
        off_copy[3].wait()
        for t in (0, 1):
            tall_put(pb.at[t], 1, 0, product(0, 4, 3, t, 0))

        def half(t):
            for _ in row_reduce(t, 1, 3, False):
                yield 1
            for level in (3, 2, 1):
                m = MEMBERS[level] // 2
                if t == 0:
                    inv_copy[level].wait()
                solve(t, m, level)
                for _ in col_reduce(t, m):
                    yield 1

                def near(i, level=level, m=m):
                    j = t * 2 * m + i
                    value = product(t, level, level - 1, j, i // 2)
                    tall_put(pb.at[t], 2 * m, i, value + upward[NODE[level - 1] + j])

                each(2 * m, near)
                steps = row_reduce(t, 2 * m, level - 1, False)
                next(steps)
                yield 1
                for under in range(level - 2, -1, -1):

                    def far(i, level=level, m=m, under=under):
                        j = t * (MEMBERS[under] // 2) + i
                        value = product(t, level, under, j, i // 2 ** (level - under))
                        upward[NODE[under] + j] = value + upward[NODE[under] + j]

                    each(MEMBERS[under] // 2, far)
                show(t, m, level)
                yield 1
                for _ in steps:
                    yield 1
            if t == 0:
                inv_copy[0].wait()
            for j in range(8):
                v = dot(ui[t * 8 + j], tall_get(xb.at[t], 8, j))
                for h in (0, 1):
                    wide[h, pl.ds(t * 8 + j, LOW, stride=16), :] = v[:, h * H : (h + 1) * H]

        halves = [half(0), half(1)]
        for g in halves:
            next(g)
        for h in (0, 1):
            topb[h, :, :] = lowb[0, h, 0:PITCH, :]

        def root_part(under, first, n):
            def one(i):
                j = first + i
                slot = SLOT[under] + j * (LEVELS - 1 - under) + 3 - under
                scale = present[slot].astype(F32)
                upward[NODE[under] + j] = scale * dot_first(uo[slot], low_get(topb, 0))

            each(n, one)

        def root_far():
            for under in (2, 1, 0):
                off_copy[under].wait()
                for first in range(0, MEMBERS[under], 4):
                    root_part(under, first, 4)
                    if (under, first) != (0, 12):
                        if (under, first) != (0, 8):
                            yield 1
            yield 1

        show(0, 1, 4)
        run(halves + [root_far()])

        first = []
        for h in (0, 1):
            for c in range(8):
                sp[h, c // 2, c % 2] = wide[h, pl.ds(c * SHARES, SHARES), :].astype(BF)
            first.append(send(sp.at[h, :, 1 - core], crs.at[h], FC + h, sibling))
        second = []
        for h in (0, 1):
            wait([first[h]])
            copies = []
            for d in (2, 1, 3):
                to = (y + d) % 4
                fys[h, to] = (sp[h, to, core].astype(F32) + crs[h, to].astype(F32)).astype(BF)
                copies.append(send(fys.at[h, to], fyr.at[h, d - 1], FY + h * 3 + d - 1, ypeer(d)))
            second.append(copies)

        def move(i):
            at = pl.ds(pl.multiple_of(i * 16, 16), 16)
            to = pl.ds(pl.multiple_of(i * 32 + 16, 16), 16)
            for h in (0, 1):
                out[to, h * H : (h + 1) * H] = shown[h, at, :]

        each(SMALL, move)
        for h in (0, 1):
            wait(second[h])

            def finish(i, h=h):
                at = pl.ds(pl.multiple_of(i * 16, 16), 16)
                s = sp[h, y, core, at, :].astype(F32) + crs[h, y, at, :].astype(F32)
                for k in range(3):
                    s = s + fyr[h, k, at, :].astype(F32)
                out[pl.ds(pl.multiple_of(i * 32, 32), 16), h * H : (h + 1) * H] = s

            each(SMALL, finish)

    pl.run_scoped(
        backward_sweep,
        pltpu.VMEM((K, LOW, TALL), BF),
        pltpu.VMEM((NOFF, LOW, TALL), BF),
        pltpu.VMEM((30, TALL, R), F32),
    )


def on_device(right_sides, lower_inv, lower_off, upper_inv, upper_off, present):
    vmem = pl.BlockSpec(memory_space=pltpu.VMEM)
    hbm = pl.BlockSpec(memory_space=pl.ANY)
    out = pl.pallas_call(
        kernel,
        out_shape=jax.ShapeDtypeStruct((32 * SMALL, R), F32),
        in_specs=[vmem, pl.BlockSpec(memory_space=pltpu.SMEM), hbm, hbm, hbm, hbm],
        out_specs=vmem,
        scratch_shapes=[
            pltpu.VMEM((2, 2, 4, 608, H), BF),
            pltpu.VMEM((2, 2, 3, 608, H), BF),
            pltpu.VMEM((2, 2, 608, H), BF),
            pltpu.VMEM((2, 2, 3, 608, H), BF),
            pltpu.VMEM((2, 2, 4, 608, H), BF),
            pltpu.VMEM((2, 2, FWROWS, H), F32),
            pltpu.VMEM((2, 2, 608, H), F32),
            pltpu.VMEM((2, 2, 4 * PITCH, H), BF),
            pltpu.VMEM((2, 4 * PITCH, H), BF),
            pltpu.VMEM((2, 4 * PITCH, H), F32),
            pltpu.VMEM((2, 4 * PITCH, H), BF),
            pltpu.VMEM((2, 2, 3, 4 * PITCH, H), BF),
            pltpu.VMEM((2, 2, 8 * PITCH, H), BF),
            pltpu.VMEM((2, PITCH, H), BF),
            pltpu.VMEM((2, 15 * PITCH, H), BF),
            pltpu.VMEM((2, 4, 2, SMALL, 16, H), BF),
            pltpu.VMEM((2, 4, 2, SMALL, 16, H), BF),
            pltpu.VMEM((2, 8 * SHARES, H), F32),
            pltpu.VMEM((2, SHARES, H), F32),
            pltpu.VMEM((2, 4, 2, SHARES, H), BF),
            pltpu.VMEM((2, 4, SHARES, H), BF),
            pltpu.VMEM((2, 4, SHARES, H), BF),
            pltpu.VMEM((2, 3, SHARES, H), BF),
            pltpu.SemaphoreType.DMA((NSEM,)),
            pltpu.SemaphoreType.DMA((NSEM,)),
            pltpu.SemaphoreType.DMA((9,)),
        ],
        compiler_params=pltpu.CompilerParams(
            collective_id=0, has_side_effects=True, vmem_limit_bytes=60 * 1024 * 1024
        ),
    )(
        jnp.swapaxes(right_sides, 0, 1),
        present,
        jnp.swapaxes(lower_inv, 1, 2),
        lower_off,
        upper_inv,
        jnp.swapaxes(upper_off, 1, 2),
    )
    return jnp.swapaxes(out.reshape(SMALL, 32, R)[:, :K], 0, 1)


def solution(mesh):
    placed = (
        P(None, ("row", "col"), None),
        P(None, "col", "row"),
        P(None, "row", "col"),
        P(None, "row", "col"),
        P(None, "col", "row"),
        P(),
    )
    return jax.shard_map(
        on_device,
        mesh=mesh,
        in_specs=placed,
        out_specs=P(None, ("row", "col"), None),
        check_vma=False,
    )
```

```python
import jax
import jax.numpy as jnp
from jax import lax
from jax.experimental import pallas as pl
from jax.experimental.pallas import tpu as pltpu
from jax.sharding import PartitionSpec as P

LEVELS = 5
K = 31
NOFF = 98
R = 256
H = 128
TALL = 304
LOW = 152
PITCH = 160
SMALL = 19
GROUP = 152
MEMBERS = [16, 8, 4, 2, 1]
NODE = [0, 16, 24, 28, 30]
SLOT = [0, 64, 88, 96, 98]
PIECE = {8: 608, 4: 304, 2: 160, 1: 80}
FWROW = [0, 608, 912, 1072, 1152]
FWROWS = 1232
MESH = pl.DeviceIdType.MESH
BF = jnp.bfloat16
F32 = jnp.float32

RS, EX, AG, CR, CG, YX, HALF = 0, 6, 12, 18, 19, 20, 26
IY, IC, FC, FY = 52, 76, 84, 88
NSEM = 100


def dot(a, b):
    return jnp.dot(a, b, preferred_element_type=F32)


def dot_first(a, b):
    return lax.dot_general(a, b, (((0,), (0,)), ((), ())), preferred_element_type=F32)


def kernel(
    rs, present, linv, loff, uinv, uoff, out,
    pb, rb, es, eb, xb, fw, tot, cb, crb, ct, ys, yb, lowb, topb, rg, ag, wide, shown, sp, crs, fys, fyr,
    ssem, rsem, wsem,
):
    row, col = lax.axis_index("row"), lax.axis_index("col")
    z, x = row // 4, row % 4
    y, core = col // 2, col % 2
    sibling = (row, y * 2 + 1 - core)
    along = (z, x)

    def zpeer(d):
        return (((z + d) % 4) * 4 + x, col)

    def xpeer(d):
        return (z * 4 + (x + d) % 4, col)

    def ypeer(d):
        return (row, ((y + d) % 4) * 2 + core)

    first_peer = (zpeer, xpeer)
    second_peer = (xpeer, zpeer)

    for h in (0, 1):
        part = slice(h * H, (h + 1) * H)
        ends = jnp.concatenate([rs[:, 16:31, part], jnp.zeros((SMALL, 1, H), BF)], axis=1)
        for g in range(4):
            v = (rs[:, 0:16, part] if g < 2 else ends).astype(F32)
            v = v[:, 8 * (g % 2) : 8 * (g % 2) + 8, :].reshape(GROUP, H)
            ag[g, h, y, core, 0:GROUP, :] = v.astype(BF)

    barrier = pltpu.get_barrier_semaphore()
    for d in (1, 2, 3):
        for peer in (zpeer, xpeer, ypeer):
            pl.semaphore_signal(barrier, inc=1, device_id=peer(d), device_id_type=MESH)
    pl.semaphore_signal(barrier, inc=1, device_id=sibling, device_id_type=MESH)
    pl.semaphore_wait(barrier, 10)

    def send(src, dst, sem, to):
        c = pltpu.make_async_remote_copy(
            src, dst, ssem.at[sem], rsem.at[sem], device_id=to, device_id_type=MESH
        )
        c.start()
        return c

    def wait(copies):
        for c in copies:
            c.wait()

    def chunks(rows, chunk, body):
        if rows == chunk:
            body(pl.ds(0, chunk), 0)
        else:

            def step(i, _):
                at = pl.multiple_of(i * chunk, 16)
                body(pl.ds(at, chunk), at)
                return 0

            lax.fori_loop(0, rows // chunk, step, 0)

    def each(n, body):
        if n <= 2:
            for i in range(n):
                body(i)
        else:

            def step(i, _):
                body(i)
                return 0

            lax.fori_loop(0, n, step, 0, unroll=2 if n % 2 == 0 else 1)

    def tall_get(ref, m, j):
        if m >= 4:
            per = m // 4
            q, at = j // per, (j % per) * TALL
            if not isinstance(at, int):
                at = pl.multiple_of(at, 16)
            halves = [ref[h, q, pl.ds(at, TALL), :] for h in (0, 1)]
        elif m == 2:
            halves = [
                jnp.concatenate([ref[h, 2 * j, 0:160, :], ref[h, 2 * j + 1, 0:144, :]], axis=0)
                for h in (0, 1)
            ]
        else:
            halves = [
                jnp.concatenate(
                    [ref[h, q, 0:80, :] for q in range(3)] + [ref[h, 3, 0:64, :]], axis=0
                )
                for h in (0, 1)
            ]
        return jnp.concatenate(halves, axis=1)

    def tall_put(ref, m, j, value):
        value = value.astype(BF)
        for h in (0, 1):
            v = value[:, h * H : (h + 1) * H]
            if m >= 4:
                per = m // 4
                q, at = j // per, (j % per) * TALL
                if not isinstance(at, int):
                    at = pl.multiple_of(at, 16)
                ref[h, q, pl.ds(at, TALL), :] = v
            elif m == 2:
                ref[h, 2 * j, 0:160, :] = v[0:160]
                ref[h, 2 * j + 1, 0:144, :] = v[160:304]
            else:
                for q in range(3):
                    ref[h, q, 0:80, :] = v[80 * q : 80 * q + 80]
                ref[h, 3, 0:64, :] = v[240:304]

    def low_rows(j):
        at = j * PITCH
        return pl.ds(at if isinstance(at, int) else pl.multiple_of(at, 16), LOW)

    def low_get(ref, j):
        return jnp.concatenate([ref[h, low_rows(j), :] for h in (0, 1)], axis=1)

    def low_put(ref, j, value):
        value = value.astype(BF)
        for h in (0, 1):
            ref[h, low_rows(j), :] = value[:, h * H : (h + 1) * H]

    def row_reduce(t, m, level, forward):
        rows, base, sem = PIECE[m], FWROW[level], HALF * t
        chunk = min(rows, TALL)
        first = [
            [
                send(
                    pb.at[t, h, (along[h] + d) % 4, pl.ds(0, rows)],
                    rb.at[t, h, d - 1, pl.ds(0, rows)],
                    sem + RS + h * 3 + d - 1,
                    first_peer[h](d),
                )
                for d in (2, 1, 3)
            ]
            for h in (0, 1)
        ]
        yield
        second = []
        for h in (0, 1):
            wait(first[h])

            def add(at, _, h=h):
                s = pb[t, h, along[h], at, :].astype(F32)
                for k in range(3):
                    s = s + rb[t, h, k, at, :].astype(F32)
                tot[t, h, at, :] = s
                es[t, h, at, :] = s.astype(BF)

            chunks(rows, chunk, add)
            second.append(
                [
                    send(
                        es.at[t, h, pl.ds(0, rows)],
                        eb.at[t, h, d - 1, pl.ds(0, rows)],
                        sem + EX + h * 3 + d - 1,
                        second_peer[h](d),
                    )
                    for d in (2, 1, 3)
                ]
            )
        yield
        third = []
        for h in (0, 1):
            wait(second[h])

            def last(at, start, h=h):
                s = tot[t, h, at, :]
                for k in range(3):
                    s = s + eb[t, h, k, at, :].astype(F32)
                kept = pl.ds(
                    base + start if isinstance(start, int) else pl.multiple_of(base + start, 16),
                    chunk,
                )
                if forward:
                    fw[t, h, kept, :] = s
                else:
                    s = fw[t, h, kept, :] - s
                xb[t, h, along[h], at, :] = s.astype(BF)

            chunks(rows, chunk, last)
            mine = xb.at[t, h, along[h], pl.ds(0, rows)]
            third.append(
                [send(mine, mine, sem + AG + h * 3 + d - 1, first_peer[h](d)) for d in (2, 1, 3)]
            )
        yield
        for h in (0, 1):
            wait(third[h])

    turns = [0, 0]

    def col_reduce(t, m, base=None, aside=None):
        rows, sem, turn = m * PITCH, HALF * t, turns[t]
        turns[t] = 1 - turn
        copies = [
            send(cb.at[t, 1 - core, pl.ds(0, rows)], crb.at[t, pl.ds(0, rows)], sem + CR, sibling)
        ]
        yield
        wait(copies)

        def add(at, _):
            s = cb[t, core, at, :].astype(F32) + crb[t, at, :].astype(F32)
            ct[t, at, :] = s
            ys[t, at, :] = s.astype(BF)

        chunks(rows, PITCH, add)
        copies = [
            send(
                ys.at[t, pl.ds(0, rows)],
                yb.at[t, turn, d - 1, pl.ds(0, rows)],
                sem + YX + turn * 3 + d - 1,
                ypeer(d),
            )
            for d in (2, 1, 3)
        ]
        if aside is not None:
            yield
            aside()
        yield
        wait(copies)

        def last(at, start):
            s = ct[t, at, :]
            for k in range(3):
                s = s + yb[t, turn, k, at, :].astype(F32)
            if base is not None:
                first = base + start
                if not isinstance(start, int):
                    first = pl.multiple_of(first, 16)
                s = rg[core, pl.ds(first, PITCH), :].astype(F32) - s
            lowb[t, core, at, :] = s.astype(BF)

        chunks(rows, PITCH, last)
        mine = lowb.at[t, core, pl.ds(0, rows)]
        copies = [send(mine, mine, sem + CG, sibling)]
        yield
        wait(copies)

    def gather_y(g):
        return [
            [
                send(
                    ag.at[g, h, y, core],
                    ag.at[g, h, y, core],
                    IY + g * 6 + h * 3 + d - 1,
                    ypeer(d),
                )
                for d in (2, 1, 3)
            ]
            for h in (0, 1)
        ]

    def gather_core(g, copies):
        more = []
        for h in (0, 1):
            wait(copies[h])
            mine = ag.at[g, h, :, core]
            more.append(send(mine, mine, IC + g * 2 + h, sibling))
        return more

    def unpack(g, copies, members, place):
        t = g % 2
        for h in (0, 1):
            wait([copies[h]])
            for c in range(8):
                v = ag[g, h, c // 2, c % 2, 0:GROUP, :].astype(F32)
                wide[t, h, pl.ds(c * GROUP, GROUP), :] = v
            for j in range(members):
                v = wide[t, h, pl.ds(j, LOW, stride=8), :]
                place(h, j, v.astype(BF))

    def col_steps(*args):
        for _ in col_reduce(*args):
            yield 1

    def row_steps(*args):
        for _ in row_reduce(*args):
            yield 1

    def run(halves):
        halves = list(halves)
        while halves:
            for g in list(halves):
                if next(g, 0) == 0:
                    halves.remove(g)

    def fetch(src, dst, first, n, sem):
        c = pltpu.make_async_copy(src.at[pl.ds(first, n)], dst.at[pl.ds(first, n)], wsem.at[sem])
        c.start()
        return c

    def forward_sweep(li, lo, waiting):
        inv_copy, off_copy = [], []
        gathers = [gather_y(g) for g in range(4)]
        for level in range(LEVELS):
            inv_copy.append(fetch(linv, li, NODE[level], MEMBERS[level], level))
            if level < 4:
                off_copy.append(
                    fetch(loff, lo, SLOT[level], SLOT[level + 1] - SLOT[level], 5 + level)
                )
        waiting[...] = jnp.zeros_like(waiting)

        def solve(t, m, level):
            first = NODE[level] + t * m

            def one(j):
                tall_put(pb.at[t], m, j, dot_first(li[first + j], low_get(lowb.at[t], j)))

            each(m, one)

        def product(t, m, level, j, a):
            above = LEVELS - 1 - level
            slot = SLOT[level] + (t * m + j) * above + a - 1
            scale = present[slot].astype(F32)
            return scale * dot(lo[slot], tall_get(xb.at[t], m, j))

        def half(t):
            def leaves(h, j, v):
                lowb[t, h, low_rows(j), :] = v

            unpack(t, gather_core(t, gathers[t]), 8, leaves)
            for level in range(4):
                m = MEMBERS[level] // 2
                above = LEVELS - 1 - level
                if t == 0:
                    inv_copy[level].wait()
                solve(t, m, level)
                for _ in row_reduce(t, m, level, True):
                    yield 1
                if t == 0:
                    off_copy[level].wait()
                if level == 3:
                    break
                to = NODE[level + 1] - 16 + t * (m // 2)

                def near(k, level=level, m=m, to=to):
                    value = product(t, m, level, 2 * k, 1) + product(t, m, level, 2 * k + 1, 1)
                    if level > 0:
                        value = value + waiting[to + k]
                    low_put(cb.at[t], k, value)

                each(m // 2, near)

                def far(level=level, m=m, above=above):
                    def one(j):
                        for a in range(2, above + 1):
                            k = NODE[level + a] - 16 + (t * m + j) // 2**a
                            waiting[k] = waiting[k] + product(t, m, level, j, a)

                    each(m, one)

                for _ in col_reduce(t, m // 2, to * PITCH, far):
                    yield 1

        halves = [half(0), half(1)]
        for g in halves:
            next(g)
        for g in (2, 3):

            def others(h, j, v, g=g):
                rg[h, low_rows(8 * (g - 2) + j), :] = v

            unpack(g, gather_core(g, gathers[g]), 8 if g == 2 else 7, others)
        run(halves)
        low_put(cb.at[0], 0, waiting[14] + product(0, 1, 3, 0, 1) + product(1, 1, 3, 0, 1))
        run([col_steps(0, 1, 14 * PITCH)])
        inv_copy[4].wait()
        solve(0, 1, 4)
        run([row_steps(0, 1, 4, True)])

    pl.run_scoped(
        forward_sweep,
        pltpu.VMEM((K, LOW, TALL), BF),
        pltpu.VMEM((NOFF, LOW, TALL), BF),
        pltpu.VMEM((15, LOW, R), F32),
    )

    def backward_sweep(ui, uo, upward):
        spot = lax.broadcasted_iota(jnp.int32, (24, LOW), 1)
        at_row = lax.broadcasted_iota(jnp.int32, (24, LOW), 0) + col * SMALL
        own = jnp.where(spot == at_row, 1.0, 0.0).astype(BF)
        inv_copy, off_copy = {}, {}
        for level in reversed(range(LEVELS)):
            if level < 4:
                off_copy[level] = fetch(
                    uoff, uo, SLOT[level], SLOT[level + 1] - SLOT[level], 5 + level
                )
            inv_copy[level] = fetch(uinv, ui, NODE[level], MEMBERS[level], level)

        def solve(t, m, level):
            first = NODE[level] + t * m

            def one(j):
                low_put(cb.at[t], j, dot(ui[first + j], tall_get(xb.at[t], m, j)))

            each(m, one)

        def product(t, level, under, j, k):
            slot = SLOT[under] + j * (LEVELS - 1 - under) + level - under - 1
            scale = present[slot].astype(F32)
            return scale * dot_first(uo[slot], low_get(lowb.at[t], k))

        def show(t, m, level):
            for j in range(m):
                v = dot(own, low_get(lowb.at[t], j))[:SMALL]
                for h in (0, 1):
                    shown[h, pl.ds(NODE[level] - 16 + t * m + j, SMALL, stride=16), :] = v[
                        :, h * H : (h + 1) * H
                    ]

        inv_copy[4].wait()
        solve(0, 1, 4)
        run([col_steps(0, 1)])
        off_copy[3].wait()
        for t in (0, 1):
            tall_put(pb.at[t], 1, 0, product(0, 4, 3, t, 0))

        def half(t):
            for _ in row_reduce(t, 1, 3, False):
                yield 1
            for level in (3, 2, 1):
                m = MEMBERS[level] // 2
                if t == 0:
                    inv_copy[level].wait()
                solve(t, m, level)
                for _ in col_reduce(t, m):
                    yield 1

                def near(i, level=level, m=m):
                    j = t * 2 * m + i
                    value = product(t, level, level - 1, j, i // 2)
                    tall_put(pb.at[t], 2 * m, i, value + upward[NODE[level - 1] + j])

                each(2 * m, near)
                steps = row_reduce(t, 2 * m, level - 1, False)
                next(steps)
                yield 1
                for under in range(level - 2, -1, -1):

                    def far(i, level=level, m=m, under=under):
                        j = t * (MEMBERS[under] // 2) + i
                        value = product(t, level, under, j, i // 2 ** (level - under))
                        upward[NODE[under] + j] = value + upward[NODE[under] + j]

                    each(MEMBERS[under] // 2, far)
                show(t, m, level)
                yield 1
                for _ in steps:
                    yield 1
            if t == 0:
                inv_copy[0].wait()
            for j in range(8):
                v = dot(ui[t * 8 + j], tall_get(xb.at[t], 8, j))
                for h in (0, 1):
                    wide[t, h, pl.ds(j, LOW, stride=8), :] = v[:, h * H : (h + 1) * H]
            first = []
            for h in (0, 1):
                for c in range(8):
                    v = wide[t, h, pl.ds(c * GROUP, GROUP), :]
                    sp[t, h, c // 2, c % 2, 0:GROUP, :] = v.astype(BF)
                first.append(
                    send(sp.at[t, h, :, 1 - core], crs.at[t, h], FC + t * 2 + h, sibling)
                )
            yield 1
            second = []
            for h in (0, 1):
                wait([first[h]])
                copies = []
                for d in (2, 1, 3):
                    to = (y + d) % 4
                    v = sp[t, h, to, core].astype(F32) + crs[t, h, to].astype(F32)
                    fys[t, h, to] = v.astype(BF)
                    copies.append(
                        send(
                            fys.at[t, h, to],
                            fyr.at[t, h, d - 1],
                            FY + t * 6 + h * 3 + d - 1,
                            ypeer(d),
                        )
                    )
                second.append(copies)
            yield 1
            if t == 0:
                for i in range(SMALL):
                    for h in (0, 1):
                        v = shown[h, pl.ds(i * 16, 16), :]
                        out[pl.ds(i * 32 + 16, 16), h * H : (h + 1) * H] = v
            for h in (0, 1):
                wait(second[h])
                v = sp[t, h, y, core].astype(F32) + crs[t, h, y].astype(F32)
                for k in range(3):
                    v = v + fyr[t, h, k].astype(F32)
                for i in range(SMALL):
                    out[pl.ds(i * 32 + t * 8, 8), h * H : (h + 1) * H] = v[8 * i : 8 * i + 8]

        halves = [half(0), half(1)]
        for g in halves:
            next(g)
        for h in (0, 1):
            topb[h, :, :] = lowb[0, h, 0:PITCH, :]

        def root_part(under, first, n):
            def one(i):
                j = first + i
                slot = SLOT[under] + j * (LEVELS - 1 - under) + 3 - under
                scale = present[slot].astype(F32)
                upward[NODE[under] + j] = scale * dot_first(uo[slot], low_get(topb, 0))

            each(n, one)

        def root_far():
            for under in (2, 1, 0):
                off_copy[under].wait()
                for first in range(0, MEMBERS[under], 4):
                    root_part(under, first, 4)
                    if (under, first) != (0, 12):
                        if (under, first) != (0, 8):
                            yield 1
            yield 1

        show(0, 1, 4)
        run(halves + [root_far()])

    pl.run_scoped(
        backward_sweep,
        pltpu.VMEM((K, LOW, TALL), BF),
        pltpu.VMEM((NOFF, LOW, TALL), BF),
        pltpu.VMEM((30, TALL, R), F32),
    )


def on_device(right_sides, lower_inv, lower_off, upper_inv, upper_off, present):
    vmem = pl.BlockSpec(memory_space=pltpu.VMEM)
    hbm = pl.BlockSpec(memory_space=pl.ANY)
    out = pl.pallas_call(
        kernel,
        out_shape=jax.ShapeDtypeStruct((32 * SMALL, R), F32),
        in_specs=[vmem, pl.BlockSpec(memory_space=pltpu.SMEM), hbm, hbm, hbm, hbm],
        out_specs=vmem,
        scratch_shapes=[
            pltpu.VMEM((2, 2, 4, 608, H), BF),
            pltpu.VMEM((2, 2, 3, 608, H), BF),
            pltpu.VMEM((2, 2, 608, H), BF),
            pltpu.VMEM((2, 2, 3, 608, H), BF),
            pltpu.VMEM((2, 2, 4, 608, H), BF),
            pltpu.VMEM((2, 2, FWROWS, H), F32),
            pltpu.VMEM((2, 2, 608, H), F32),
            pltpu.VMEM((2, 2, 4 * PITCH, H), BF),
            pltpu.VMEM((2, 4 * PITCH, H), BF),
            pltpu.VMEM((2, 4 * PITCH, H), F32),
            pltpu.VMEM((2, 4 * PITCH, H), BF),
            pltpu.VMEM((2, 2, 3, 4 * PITCH, H), BF),
            pltpu.VMEM((2, 2, 8 * PITCH, H), BF),
            pltpu.VMEM((2, PITCH, H), BF),
            pltpu.VMEM((2, 15 * PITCH, H), BF),
            pltpu.VMEM((4, 2, 4, 2, PITCH, H), BF),
            pltpu.VMEM((2, 2, 8 * GROUP + 16, H), F32),
            pltpu.VMEM((2, 25 * 16, H), F32),
            pltpu.VMEM((2, 2, 4, 2, PITCH, H), BF),
            pltpu.VMEM((2, 2, 4, PITCH, H), BF),
            pltpu.VMEM((2, 2, 4, PITCH, H), BF),
            pltpu.VMEM((2, 2, 3, PITCH, H), BF),
            pltpu.SemaphoreType.DMA((NSEM,)),
            pltpu.SemaphoreType.DMA((NSEM,)),
            pltpu.SemaphoreType.DMA((9,)),
        ],
        compiler_params=pltpu.CompilerParams(
            collective_id=0, has_side_effects=True, vmem_limit_bytes=60 * 1024 * 1024
        ),
    )(
        jnp.swapaxes(right_sides, 0, 1),
        present,
        jnp.swapaxes(lower_inv, 1, 2),
        lower_off,
        upper_inv,
        jnp.swapaxes(upper_off, 1, 2),
    )
    return jnp.swapaxes(out.reshape(SMALL, 32, R)[:, :K], 0, 1)


def solution(mesh):
    placed = (
        P(None, ("row", "col"), None),
        P(None, "col", "row"),
        P(None, "row", "col"),
        P(None, "row", "col"),
        P(None, "col", "row"),
        P(),
    )
    return jax.shard_map(
        on_device,
        mesh=mesh,
        in_specs=placed,
        out_specs=P(None, ("row", "col"), None),
        check_vma=False,
    )
```

```python
import jax
import jax.numpy as jnp
from jax import lax
from jax.experimental import pallas as pl
from jax.experimental.pallas import tpu as pltpu
from jax.sharding import PartitionSpec as P

LEVELS = 5
K = 31
NOFF = 98
R = 256
H = 128
TALL = 304
LOW = 152
PITCH = 160
SMALL = 19
GROUP = 152
MEMBERS = [16, 8, 4, 2, 1]
NODE = [0, 16, 24, 28, 30]
SLOT = [0, 64, 88, 96, 98]
PIECE = {8: 608, 4: 304, 2: 160, 1: 80}
FWROW = [0, 608, 912, 1072, 1152]
FWROWS = 1232
MESH = pl.DeviceIdType.MESH
BF = jnp.bfloat16
F32 = jnp.float32

RS, EX, AG, CR, CG, YX, HALF = 0, 6, 12, 18, 19, 20, 26
IY, IC, FC, FY = 52, 76, 84, 88
NSEM = 100


def dot(a, b):
    return jnp.dot(a, b, preferred_element_type=F32)


def dot_first(a, b):
    return lax.dot_general(a, b, (((0,), (0,)), ((), ())), preferred_element_type=F32)


def kernel(
    rs, present, linv, loff, uinv, uoff, out,
    pb, rb, es, eb, xb, fw, tot, cb, crb, ct, ys, yb, lowb, topb, rg, ag, wide, shown, sp, crs, fys, fyr,
    ssem, rsem, wsem,
):
    row, col = lax.axis_index("row"), lax.axis_index("col")
    z, x = row // 4, row % 4
    y, core = col // 2, col % 2
    sibling = (row, y * 2 + 1 - core)
    along = (z, x)

    def zpeer(d):
        return (((z + d) % 4) * 4 + x, col)

    def xpeer(d):
        return (z * 4 + (x + d) % 4, col)

    def ypeer(d):
        return (row, ((y + d) % 4) * 2 + core)

    first_peer = (zpeer, xpeer)
    second_peer = (xpeer, zpeer)

    for h in (0, 1):
        part = slice(h * H, (h + 1) * H)
        ends = jnp.concatenate([rs[:, 16:31, part], jnp.zeros((SMALL, 1, H), BF)], axis=1)
        for g in range(4):
            v = (rs[:, 0:16, part] if g < 2 else ends).astype(F32)
            v = v[:, 8 * (g % 2) : 8 * (g % 2) + 8, :].reshape(GROUP, H)
            ag[g, h, y, core, 0:GROUP, :] = v.astype(BF)

    barrier = pltpu.get_barrier_semaphore()
    for d in (1, 2, 3):
        for peer in (zpeer, xpeer, ypeer):
            pl.semaphore_signal(barrier, inc=1, device_id=peer(d), device_id_type=MESH)
    pl.semaphore_signal(barrier, inc=1, device_id=sibling, device_id_type=MESH)
    pl.semaphore_wait(barrier, 10)

    def send(src, dst, sem, to):
        c = pltpu.make_async_remote_copy(
            src, dst, ssem.at[sem], rsem.at[sem], device_id=to, device_id_type=MESH
        )
        c.start()
        return c

    def wait(copies):
        for c in copies:
            c.wait()

    def chunks(rows, chunk, body):
        if rows == chunk:
            body(pl.ds(0, chunk), 0)
        else:

            def step(i, _):
                at = pl.multiple_of(i * chunk, 16)
                body(pl.ds(at, chunk), at)
                return 0

            lax.fori_loop(0, rows // chunk, step, 0)

    def each(n, body):
        if n <= 2:
            for i in range(n):
                body(i)
        else:

            def step(i, _):
                body(i)
                return 0

            lax.fori_loop(0, n, step, 0, unroll=4 if n % 4 == 0 else 1)

    def tall_get(ref, m, j):
        if m >= 4:
            per = m // 4
            q, at = j // per, (j % per) * TALL
            if not isinstance(at, int):
                at = pl.multiple_of(at, 16)
            halves = [ref[h, q, pl.ds(at, TALL), :] for h in (0, 1)]
        elif m == 2:
            halves = [
                jnp.concatenate([ref[h, 2 * j, 0:160, :], ref[h, 2 * j + 1, 0:144, :]], axis=0)
                for h in (0, 1)
            ]
        else:
            halves = [
                jnp.concatenate(
                    [ref[h, q, 0:80, :] for q in range(3)] + [ref[h, 3, 0:64, :]], axis=0
                )
                for h in (0, 1)
            ]
        return jnp.concatenate(halves, axis=1)

    def tall_put(ref, m, j, value):
        value = value.astype(BF)
        for h in (0, 1):
            v = value[:, h * H : (h + 1) * H]
            if m >= 4:
                per = m // 4
                q, at = j // per, (j % per) * TALL
                if not isinstance(at, int):
                    at = pl.multiple_of(at, 16)
                ref[h, q, pl.ds(at, TALL), :] = v
            elif m == 2:
                ref[h, 2 * j, 0:160, :] = v[0:160]
                ref[h, 2 * j + 1, 0:144, :] = v[160:304]
            else:
                for q in range(3):
                    ref[h, q, 0:80, :] = v[80 * q : 80 * q + 80]
                ref[h, 3, 0:64, :] = v[240:304]

    def low_rows(j):
        at = j * PITCH
        return pl.ds(at if isinstance(at, int) else pl.multiple_of(at, 16), LOW)

    def low_get(ref, j):
        return jnp.concatenate([ref[h, low_rows(j), :] for h in (0, 1)], axis=1)

    def low_put(ref, j, value):
        value = value.astype(BF)
        for h in (0, 1):
            ref[h, low_rows(j), :] = value[:, h * H : (h + 1) * H]

    def row_reduce(t, m, level, forward):
        rows, base, sem = PIECE[m], FWROW[level], HALF * t
        chunk = min(rows, TALL)
        first = [
            [
                send(
                    pb.at[t, h, (along[h] + d) % 4, pl.ds(0, rows)],
                    rb.at[t, h, d - 1, pl.ds(0, rows)],
                    sem + RS + h * 3 + d - 1,
                    first_peer[h](d),
                )
                for d in (2, 1, 3)
            ]
            for h in (0, 1)
        ]
        yield
        second = []
        for h in (0, 1):
            wait(first[h])

            def add(at, _, h=h):
                s = pb[t, h, along[h], at, :].astype(F32)
                for k in range(3):
                    s = s + rb[t, h, k, at, :].astype(F32)
                tot[t, h, at, :] = s
                es[t, h, at, :] = s.astype(BF)

            chunks(rows, chunk, add)
            second.append(
                [
                    send(
                        es.at[t, h, pl.ds(0, rows)],
                        eb.at[t, h, d - 1, pl.ds(0, rows)],
                        sem + EX + h * 3 + d - 1,
                        second_peer[h](d),
                    )
                    for d in (2, 1, 3)
                ]
            )
        yield
        third = []
        for h in (0, 1):
            wait(second[h])

            def last(at, start, h=h):
                s = tot[t, h, at, :]
                for k in range(3):
                    s = s + eb[t, h, k, at, :].astype(F32)
                kept = pl.ds(
                    base + start if isinstance(start, int) else pl.multiple_of(base + start, 16),
                    chunk,
                )
                if forward:
                    fw[t, h, kept, :] = s
                else:
                    s = fw[t, h, kept, :] - s
                xb[t, h, along[h], at, :] = s.astype(BF)

            chunks(rows, chunk, last)
            mine = xb.at[t, h, along[h], pl.ds(0, rows)]
            third.append(
                [send(mine, mine, sem + AG + h * 3 + d - 1, first_peer[h](d)) for d in (2, 1, 3)]
            )
        yield
        for h in (0, 1):
            wait(third[h])

    turns = [0, 0]

    def col_reduce(t, m, base=None, aside=None):
        rows, sem, turn = m * PITCH, HALF * t, turns[t]
        turns[t] = 1 - turn
        copies = [
            send(cb.at[t, 1 - core, pl.ds(0, rows)], crb.at[t, pl.ds(0, rows)], sem + CR, sibling)
        ]
        yield
        wait(copies)

        def add(at, _):
            s = cb[t, core, at, :].astype(F32) + crb[t, at, :].astype(F32)
            ct[t, at, :] = s
            ys[t, at, :] = s.astype(BF)

        chunks(rows, PITCH, add)
        copies = [
            send(
                ys.at[t, pl.ds(0, rows)],
                yb.at[t, turn, d - 1, pl.ds(0, rows)],
                sem + YX + turn * 3 + d - 1,
                ypeer(d),
            )
            for d in (2, 1, 3)
        ]
        if aside is not None:
            yield
            aside()
        yield
        wait(copies)

        def last(at, start):
            s = ct[t, at, :]
            for k in range(3):
                s = s + yb[t, turn, k, at, :].astype(F32)
            if base is not None:
                first = base + start
                if not isinstance(start, int):
                    first = pl.multiple_of(first, 16)
                s = rg[core, pl.ds(first, PITCH), :].astype(F32) - s
            lowb[t, core, at, :] = s.astype(BF)

        chunks(rows, PITCH, last)
        mine = lowb.at[t, core, pl.ds(0, rows)]
        copies = [send(mine, mine, sem + CG, sibling)]
        yield
        wait(copies)

    def gather_y(g):
        return [
            [
                send(
                    ag.at[g, h, y, core],
                    ag.at[g, h, y, core],
                    IY + g * 6 + h * 3 + d - 1,
                    ypeer(d),
                )
                for d in (2, 1, 3)
            ]
            for h in (0, 1)
        ]

    def gather_core(g, copies):
        more = []
        for h in (0, 1):
            wait(copies[h])
            mine = ag.at[g, h, :, core]
            more.append(send(mine, mine, IC + g * 2 + h, sibling))
        return more

    def unpack(g, copies, members, place):
        t = g % 2
        for h in (0, 1):
            wait([copies[h]])
            for c in range(8):
                v = ag[g, h, c // 2, c % 2, 0:GROUP, :].astype(F32)
                wide[t, h, pl.ds(c * GROUP, GROUP), :] = v
            for j in range(members):
                v = wide[t, h, pl.ds(j, LOW, stride=8), :]
                place(h, j, v.astype(BF))

    def col_steps(*args):
        for _ in col_reduce(*args):
            yield 1

    def row_steps(*args):
        for _ in row_reduce(*args):
            yield 1

    def run(halves):
        halves = list(halves)
        while halves:
            for g in list(halves):
                if next(g, 0) == 0:
                    halves.remove(g)

    def fetch(src, dst, first, n, sem):
        c = pltpu.make_async_copy(src.at[pl.ds(first, n)], dst.at[pl.ds(first, n)], wsem.at[sem])
        c.start()
        return c

    def forward_sweep(li, lo, waiting):
        inv_copy, off_copy = [], []
        gathers = [gather_y(g) for g in range(4)]
        for level in range(LEVELS):
            inv_copy.append(fetch(linv, li, NODE[level], MEMBERS[level], level))
            if level < 4:
                off_copy.append(
                    fetch(loff, lo, SLOT[level], SLOT[level + 1] - SLOT[level], 5 + level)
                )
        waiting[...] = jnp.zeros_like(waiting)

        def solve(t, m, level):
            first = NODE[level] + t * m

            def one(j):
                tall_put(pb.at[t], m, j, dot_first(li[first + j], low_get(lowb.at[t], j)))

            each(m, one)

        def product(t, m, level, j, a):
            above = LEVELS - 1 - level
            slot = SLOT[level] + (t * m + j) * above + a - 1
            scale = present[slot].astype(F32)
            return scale * dot(lo[slot], tall_get(xb.at[t], m, j))

        def half(t):
            def leaves(h, j, v):
                lowb[t, h, low_rows(j), :] = v

            unpack(t, gather_core(t, gathers[t]), 8, leaves)
            for level in range(4):
                m = MEMBERS[level] // 2
                above = LEVELS - 1 - level
                if t == 0:
                    inv_copy[level].wait()
                solve(t, m, level)
                for _ in row_reduce(t, m, level, True):
                    yield 1
                if t == 0:
                    off_copy[level].wait()
                if level == 3:
                    break
                to = NODE[level + 1] - 16 + t * (m // 2)

                def near(k, level=level, m=m, to=to):
                    value = product(t, m, level, 2 * k, 1) + product(t, m, level, 2 * k + 1, 1)
                    if level > 0:
                        value = value + waiting[to + k]
                    low_put(cb.at[t], k, value)

                each(m // 2, near)

                def far(level=level, m=m, above=above):
                    def one(j):
                        for a in range(2, above + 1):
                            k = NODE[level + a] - 16 + (t * m + j) // 2**a
                            waiting[k] = waiting[k] + product(t, m, level, j, a)

                    each(m, one)

                for _ in col_reduce(t, m // 2, to * PITCH, far):
                    yield 1

        halves = [half(0), half(1)]
        for g in halves:
            next(g)
        for g in (2, 3):

            def others(h, j, v, g=g):
                rg[h, low_rows(8 * (g - 2) + j), :] = v

            unpack(g, gather_core(g, gathers[g]), 8 if g == 2 else 7, others)
        run(halves)
        low_put(cb.at[0], 0, waiting[14] + product(0, 1, 3, 0, 1) + product(1, 1, 3, 0, 1))
        run([col_steps(0, 1, 14 * PITCH)])
        inv_copy[4].wait()
        solve(0, 1, 4)
        run([row_steps(0, 1, 4, True)])

    pl.run_scoped(
        forward_sweep,
        pltpu.VMEM((K, LOW, TALL), BF),
        pltpu.VMEM((NOFF, LOW, TALL), BF),
        pltpu.VMEM((15, LOW, R), F32),
    )

    def backward_sweep(ui, uo, upward):
        spot = lax.broadcasted_iota(jnp.int32, (24, LOW), 1)
        at_row = lax.broadcasted_iota(jnp.int32, (24, LOW), 0) + col * SMALL
        own = jnp.where(spot == at_row, 1.0, 0.0).astype(BF)
        inv_copy, off_copy = {}, {}
        for level in reversed(range(LEVELS)):
            if level < 4:
                off_copy[level] = fetch(
                    uoff, uo, SLOT[level], SLOT[level + 1] - SLOT[level], 5 + level
                )
            inv_copy[level] = fetch(uinv, ui, NODE[level], MEMBERS[level], level)

        def solve(t, m, level):
            first = NODE[level] + t * m

            def one(j):
                low_put(cb.at[t], j, dot(ui[first + j], tall_get(xb.at[t], m, j)))

            each(m, one)

        def product(t, level, under, j, k):
            slot = SLOT[under] + j * (LEVELS - 1 - under) + level - under - 1
            scale = present[slot].astype(F32)
            return scale * dot_first(uo[slot], low_get(lowb.at[t], k))

        def show(t, m, level):
            for j in range(m):
                v = dot(own, low_get(lowb.at[t], j))[:SMALL]
                for h in (0, 1):
                    shown[h, pl.ds(NODE[level] - 16 + t * m + j, SMALL, stride=16), :] = v[
                        :, h * H : (h + 1) * H
                    ]

        inv_copy[4].wait()
        solve(0, 1, 4)
        run([col_steps(0, 1)])
        off_copy[3].wait()
        for t in (0, 1):
            tall_put(pb.at[t], 1, 0, product(0, 4, 3, t, 0))

        def half(t):
            for _ in row_reduce(t, 1, 3, False):
                yield 1
            for level in (3, 2, 1):
                m = MEMBERS[level] // 2
                if t == 0:
                    inv_copy[level].wait()
                solve(t, m, level)
                for _ in col_reduce(t, m):
                    yield 1

                def near(i, level=level, m=m):
                    j = t * 2 * m + i
                    value = product(t, level, level - 1, j, i // 2)
                    tall_put(pb.at[t], 2 * m, i, value + upward[NODE[level - 1] + j])

                each(2 * m, near)
                steps = row_reduce(t, 2 * m, level - 1, False)
                next(steps)
                yield 1
                for under in range(level - 2, -1, -1):

                    def far(i, level=level, m=m, under=under):
                        j = t * (MEMBERS[under] // 2) + i
                        value = product(t, level, under, j, i // 2 ** (level - under))
                        upward[NODE[under] + j] = value + upward[NODE[under] + j]

                    each(MEMBERS[under] // 2, far)
                show(t, m, level)
                yield 1
                for _ in steps:
                    yield 1
            if t == 0:
                inv_copy[0].wait()
            for j in range(8):
                v = dot(ui[t * 8 + j], tall_get(xb.at[t], 8, j))
                for h in (0, 1):
                    wide[t, h, pl.ds(j, LOW, stride=8), :] = v[:, h * H : (h + 1) * H]
            first = []
            for h in (0, 1):
                for c in range(8):
                    v = wide[t, h, pl.ds(c * GROUP, GROUP), :]
                    sp[t, h, c // 2, c % 2, 0:GROUP, :] = v.astype(BF)
                first.append(
                    send(sp.at[t, h, :, 1 - core], crs.at[t, h], FC + t * 2 + h, sibling)
                )
            yield 1
            second = []
            for h in (0, 1):
                wait([first[h]])
                copies = []
                for d in (2, 1, 3):
                    to = (y + d) % 4
                    v = sp[t, h, to, core].astype(F32) + crs[t, h, to].astype(F32)
                    fys[t, h, to] = v.astype(BF)
                    copies.append(
                        send(
                            fys.at[t, h, to],
                            fyr.at[t, h, d - 1],
                            FY + t * 6 + h * 3 + d - 1,
                            ypeer(d),
                        )
                    )
                second.append(copies)
            yield 1
            if t == 0:
                for i in range(SMALL):
                    for h in (0, 1):
                        v = shown[h, pl.ds(i * 16, 16), :]
                        out[pl.ds(i * 32 + 16, 16), h * H : (h + 1) * H] = v
            for h in (0, 1):
                wait(second[h])
                v = sp[t, h, y, core].astype(F32) + crs[t, h, y].astype(F32)
                for k in range(3):
                    v = v + fyr[t, h, k].astype(F32)
                for i in range(SMALL):
                    out[pl.ds(i * 32 + t * 8, 8), h * H : (h + 1) * H] = v[8 * i : 8 * i + 8]

        halves = [half(0), half(1)]
        for g in halves:
            next(g)
        for h in (0, 1):
            topb[h, :, :] = lowb[0, h, 0:PITCH, :]

        def root_part(under, first, n):
            def one(i):
                j = first + i
                slot = SLOT[under] + j * (LEVELS - 1 - under) + 3 - under
                scale = present[slot].astype(F32)
                upward[NODE[under] + j] = scale * dot_first(uo[slot], low_get(topb, 0))

            each(n, one)

        def root_far():
            for under in (2, 1, 0):
                off_copy[under].wait()
                for first in range(0, MEMBERS[under], 4):
                    root_part(under, first, 4)
                    if (under, first) != (0, 12):
                        if (under, first) != (0, 8):
                            yield 1
            yield 1

        show(0, 1, 4)
        run(halves + [root_far()])

    pl.run_scoped(
        backward_sweep,
        pltpu.VMEM((K, LOW, TALL), BF),
        pltpu.VMEM((NOFF, LOW, TALL), BF),
        pltpu.VMEM((30, TALL, R), F32),
    )


def on_device(right_sides, lower_inv, lower_off, upper_inv, upper_off, present):
    vmem = pl.BlockSpec(memory_space=pltpu.VMEM)
    hbm = pl.BlockSpec(memory_space=pl.ANY)
    out = pl.pallas_call(
        kernel,
        out_shape=jax.ShapeDtypeStruct((32 * SMALL, R), F32),
        in_specs=[vmem, pl.BlockSpec(memory_space=pltpu.SMEM), hbm, hbm, hbm, hbm],
        out_specs=vmem,
        scratch_shapes=[
            pltpu.VMEM((2, 2, 4, 608, H), BF),
            pltpu.VMEM((2, 2, 3, 608, H), BF),
            pltpu.VMEM((2, 2, 608, H), BF),
            pltpu.VMEM((2, 2, 3, 608, H), BF),
            pltpu.VMEM((2, 2, 4, 608, H), BF),
            pltpu.VMEM((2, 2, FWROWS, H), F32),
            pltpu.VMEM((2, 2, 608, H), F32),
            pltpu.VMEM((2, 2, 4 * PITCH, H), BF),
            pltpu.VMEM((2, 4 * PITCH, H), BF),
            pltpu.VMEM((2, 4 * PITCH, H), F32),
            pltpu.VMEM((2, 4 * PITCH, H), BF),
            pltpu.VMEM((2, 2, 3, 4 * PITCH, H), BF),
            pltpu.VMEM((2, 2, 8 * PITCH, H), BF),
            pltpu.VMEM((2, PITCH, H), BF),
            pltpu.VMEM((2, 15 * PITCH, H), BF),
            pltpu.VMEM((4, 2, 4, 2, PITCH, H), BF),
            pltpu.VMEM((2, 2, 8 * GROUP + 16, H), F32),
            pltpu.VMEM((2, 25 * 16, H), F32),
            pltpu.VMEM((2, 2, 4, 2, PITCH, H), BF),
            pltpu.VMEM((2, 2, 4, PITCH, H), BF),
            pltpu.VMEM((2, 2, 4, PITCH, H), BF),
            pltpu.VMEM((2, 2, 3, PITCH, H), BF),
            pltpu.SemaphoreType.DMA((NSEM,)),
            pltpu.SemaphoreType.DMA((NSEM,)),
            pltpu.SemaphoreType.DMA((9,)),
        ],
        compiler_params=pltpu.CompilerParams(
            collective_id=0, has_side_effects=True, vmem_limit_bytes=60 * 1024 * 1024
        ),
    )(
        jnp.swapaxes(right_sides, 0, 1),
        present,
        jnp.swapaxes(lower_inv, 1, 2),
        lower_off,
        upper_inv,
        jnp.swapaxes(upper_off, 1, 2),
    )
    return jnp.swapaxes(out.reshape(SMALL, 32, R)[:, :K], 0, 1)


def solution(mesh):
    placed = (
        P(None, ("row", "col"), None),
        P(None, "col", "row"),
        P(None, "row", "col"),
        P(None, "row", "col"),
        P(None, "col", "row"),
        P(),
    )
    return jax.shard_map(
        on_device,
        mesh=mesh,
        in_specs=placed,
        out_specs=P(None, ("row", "col"), None),
        check_vma=False,
    )
```

```python
import jax
import jax.numpy as jnp
from jax import lax
from jax.experimental import pallas as pl
from jax.experimental.pallas import tpu as pltpu
from jax.sharding import PartitionSpec as P

LEVELS = 5
K = 31
NOFF = 98
R = 256
H = 128
TALL = 304
LOW = 152
PITCH = 160
SMALL = 19
GROUP = 152
MEMBERS = [16, 8, 4, 2, 1]
NODE = [0, 16, 24, 28, 30]
SLOT = [0, 64, 88, 96, 98]
PIECE = {8: 608, 4: 304, 2: 160, 1: 80}
FWROW = [0, 608, 912, 1072, 1152]
FWROWS = 1232
MESH = pl.DeviceIdType.MESH
BF = jnp.bfloat16
F32 = jnp.float32

RS, EX, AG, CR, CG, YX, HALF = 0, 6, 12, 18, 19, 20, 26
IY, IC, FC, FY = 52, 76, 84, 88
NSEM = 100


def dot(a, b):
    return jnp.dot(a, b, preferred_element_type=F32)


def dot_first(a, b):
    return lax.dot_general(a, b, (((0,), (0,)), ((), ())), preferred_element_type=F32)


def kernel(
    rs, present, linv, loff, uinv, uoff, out,
    pb, rb, es, eb, xb, fw, tot, cb, crb, ct, ys, yb, lowb, topb, rg, ag, wide, shown, sp, crs, fys, fyr,
    ssem, rsem, wsem,
):
    row, col = lax.axis_index("row"), lax.axis_index("col")
    z, x = row // 4, row % 4
    y, core = col // 2, col % 2
    sibling = (row, y * 2 + 1 - core)
    along = (z, x)

    def zpeer(d):
        return (((z + d) % 4) * 4 + x, col)

    def xpeer(d):
        return (z * 4 + (x + d) % 4, col)

    def ypeer(d):
        return (row, ((y + d) % 4) * 2 + core)

    first_peer = (zpeer, xpeer)
    second_peer = (xpeer, zpeer)

    for h in (0, 1):
        part = slice(h * H, (h + 1) * H)
        ends = jnp.concatenate([rs[:, 16:31, part], jnp.zeros((SMALL, 1, H), BF)], axis=1)
        for g in range(4):
            v = (rs[:, 0:16, part] if g < 2 else ends).astype(F32)
            v = v[:, 8 * (g % 2) : 8 * (g % 2) + 8, :].reshape(GROUP, H)
            ag[g, h, y, core, 0:GROUP, :] = v.astype(BF)

    barrier = pltpu.get_barrier_semaphore()
    for d in (1, 2, 3):
        for peer in (zpeer, xpeer, ypeer):
            pl.semaphore_signal(barrier, inc=1, device_id=peer(d), device_id_type=MESH)
    pl.semaphore_signal(barrier, inc=1, device_id=sibling, device_id_type=MESH)
    pl.semaphore_wait(barrier, 10)

    def send(src, dst, sem, to):
        c = pltpu.make_async_remote_copy(
            src, dst, ssem.at[sem], rsem.at[sem], device_id=to, device_id_type=MESH
        )
        c.start()
        return c

    def wait(copies):
        for c in copies:
            c.wait()

    def chunks(rows, chunk, body):
        if rows == chunk:
            body(pl.ds(0, chunk), 0)
        else:

            def step(i, _):
                at = pl.multiple_of(i * chunk, 16)
                body(pl.ds(at, chunk), at)
                return 0

            lax.fori_loop(0, rows // chunk, step, 0)

    def each(n, body, unroll=8):
        if n <= 2:
            for i in range(n):
                body(i)
        else:

            def step(i, _):
                body(i)
                return 0

            lax.fori_loop(0, n, step, 0, unroll=min(n, unroll))

    def tall_get(ref, m, j):
        if m >= 4:
            per = m // 4
            q, at = j // per, (j % per) * TALL
            if not isinstance(at, int):
                at = pl.multiple_of(at, 16)
            halves = [ref[h, q, pl.ds(at, TALL), :] for h in (0, 1)]
        elif m == 2:
            halves = [
                jnp.concatenate([ref[h, 2 * j, 0:160, :], ref[h, 2 * j + 1, 0:144, :]], axis=0)
                for h in (0, 1)
            ]
        else:
            halves = [
                jnp.concatenate(
                    [ref[h, q, 0:80, :] for q in range(3)] + [ref[h, 3, 0:64, :]], axis=0
                )
                for h in (0, 1)
            ]
        return jnp.concatenate(halves, axis=1)

    def tall_put(ref, m, j, value):
        value = value.astype(BF)
        for h in (0, 1):
            v = value[:, h * H : (h + 1) * H]
            if m >= 4:
                per = m // 4
                q, at = j // per, (j % per) * TALL
                if not isinstance(at, int):
                    at = pl.multiple_of(at, 16)
                ref[h, q, pl.ds(at, TALL), :] = v
            elif m == 2:
                ref[h, 2 * j, 0:160, :] = v[0:160]
                ref[h, 2 * j + 1, 0:144, :] = v[160:304]
            else:
                for q in range(3):
                    ref[h, q, 0:80, :] = v[80 * q : 80 * q + 80]
                ref[h, 3, 0:64, :] = v[240:304]

    def low_rows(j):
        at = j * PITCH
        return pl.ds(at if isinstance(at, int) else pl.multiple_of(at, 16), LOW)

    def low_get(ref, j):
        return jnp.concatenate([ref[h, low_rows(j), :] for h in (0, 1)], axis=1)

    def low_put(ref, j, value):
        value = value.astype(BF)
        for h in (0, 1):
            ref[h, low_rows(j), :] = value[:, h * H : (h + 1) * H]

    def row_reduce(t, m, level, forward):
        rows, base, sem = PIECE[m], FWROW[level], HALF * t
        chunk = min(rows, TALL)
        first = [
            [
                send(
                    pb.at[t, h, (along[h] + d) % 4, pl.ds(0, rows)],
                    rb.at[t, h, d - 1, pl.ds(0, rows)],
                    sem + RS + h * 3 + d - 1,
                    first_peer[h](d),
                )
                for d in (2, 1, 3)
            ]
            for h in (0, 1)
        ]
        yield
        second = []
        for h in (0, 1):
            wait(first[h])

            def add(at, _, h=h):
                s = pb[t, h, along[h], at, :].astype(F32)
                for k in range(3):
                    s = s + rb[t, h, k, at, :].astype(F32)
                tot[t, h, at, :] = s
                es[t, h, at, :] = s.astype(BF)

            chunks(rows, chunk, add)
            second.append(
                [
                    send(
                        es.at[t, h, pl.ds(0, rows)],
                        eb.at[t, h, d - 1, pl.ds(0, rows)],
                        sem + EX + h * 3 + d - 1,
                        second_peer[h](d),
                    )
                    for d in (2, 1, 3)
                ]
            )
        yield
        third = []
        for h in (0, 1):
            wait(second[h])

            def last(at, start, h=h):
                s = tot[t, h, at, :]
                for k in range(3):
                    s = s + eb[t, h, k, at, :].astype(F32)
                kept = pl.ds(
                    base + start if isinstance(start, int) else pl.multiple_of(base + start, 16),
                    chunk,
                )
                if forward:
                    fw[t, h, kept, :] = s
                else:
                    s = fw[t, h, kept, :] - s
                xb[t, h, along[h], at, :] = s.astype(BF)

            chunks(rows, chunk, last)
            mine = xb.at[t, h, along[h], pl.ds(0, rows)]
            third.append(
                [send(mine, mine, sem + AG + h * 3 + d - 1, first_peer[h](d)) for d in (2, 1, 3)]
            )
        yield
        for h in (0, 1):
            wait(third[h])

    turns = [0, 0]

    def col_reduce(t, m, base=None, aside=None):
        rows, sem, turn = m * PITCH, HALF * t, turns[t]
        turns[t] = 1 - turn
        copies = [
            send(cb.at[t, 1 - core, pl.ds(0, rows)], crb.at[t, pl.ds(0, rows)], sem + CR, sibling)
        ]
        yield
        wait(copies)

        def add(at, _):
            s = cb[t, core, at, :].astype(F32) + crb[t, at, :].astype(F32)
            ct[t, at, :] = s
            ys[t, at, :] = s.astype(BF)

        chunks(rows, PITCH, add)
        copies = [
            send(
                ys.at[t, pl.ds(0, rows)],
                yb.at[t, turn, d - 1, pl.ds(0, rows)],
                sem + YX + turn * 3 + d - 1,
                ypeer(d),
            )
            for d in (2, 1, 3)
        ]
        if aside is not None:
            yield
            aside()
        yield
        wait(copies)

        def last(at, start):
            s = ct[t, at, :]
            for k in range(3):
                s = s + yb[t, turn, k, at, :].astype(F32)
            if base is not None:
                first = base + start
                if not isinstance(start, int):
                    first = pl.multiple_of(first, 16)
                s = rg[core, pl.ds(first, PITCH), :].astype(F32) - s
            lowb[t, core, at, :] = s.astype(BF)

        chunks(rows, PITCH, last)
        mine = lowb.at[t, core, pl.ds(0, rows)]
        copies = [send(mine, mine, sem + CG, sibling)]
        yield
        wait(copies)

    def gather_y(g):
        return [
            [
                send(
                    ag.at[g, h, y, core],
                    ag.at[g, h, y, core],
                    IY + g * 6 + h * 3 + d - 1,
                    ypeer(d),
                )
                for d in (2, 1, 3)
            ]
            for h in (0, 1)
        ]

    def gather_core(g, copies):
        more = []
        for h in (0, 1):
            wait(copies[h])
            mine = ag.at[g, h, :, core]
            more.append(send(mine, mine, IC + g * 2 + h, sibling))
        return more

    def unpack(g, copies, members, place):
        t = g % 2
        for h in (0, 1):
            wait([copies[h]])
            for c in range(8):
                v = ag[g, h, c // 2, c % 2, 0:GROUP, :].astype(F32)
                wide[t, h, pl.ds(c * GROUP, GROUP), :] = v
            for j in range(members):
                v = wide[t, h, pl.ds(j, LOW, stride=8), :]
                place(h, j, v.astype(BF))

    def col_steps(*args):
        for _ in col_reduce(*args):
            yield 1

    def row_steps(*args):
        for _ in row_reduce(*args):
            yield 1

    def run(halves):
        halves = list(halves)
        while halves:
            for g in list(halves):
                if next(g, 0) == 0:
                    halves.remove(g)

    def fetch(src, dst, first, n, sem):
        c = pltpu.make_async_copy(src.at[pl.ds(first, n)], dst.at[pl.ds(first, n)], wsem.at[sem])
        c.start()
        return c

    def forward_sweep(li, lo, waiting):
        inv_copy, off_copy = [], []
        gathers = [gather_y(g) for g in range(4)]
        for level in range(LEVELS):
            inv_copy.append(fetch(linv, li, NODE[level], MEMBERS[level], level))
            if level < 4:
                off_copy.append(
                    fetch(loff, lo, SLOT[level], SLOT[level + 1] - SLOT[level], 5 + level)
                )
        waiting[...] = jnp.zeros_like(waiting)

        def solve(t, m, level):
            first = NODE[level] + t * m

            def one(j):
                tall_put(pb.at[t], m, j, dot_first(li[first + j], low_get(lowb.at[t], j)))

            each(m, one)

        def product(t, m, level, j, a):
            above = LEVELS - 1 - level
            slot = SLOT[level] + (t * m + j) * above + a - 1
            scale = present[slot].astype(F32)
            return scale * dot(lo[slot], tall_get(xb.at[t], m, j))

        def half(t):
            def leaves(h, j, v):
                lowb[t, h, low_rows(j), :] = v

            unpack(t, gather_core(t, gathers[t]), 8, leaves)
            for level in range(4):
                m = MEMBERS[level] // 2
                above = LEVELS - 1 - level
                if t == 0:
                    inv_copy[level].wait()
                solve(t, m, level)
                for _ in row_reduce(t, m, level, True):
                    yield 1
                if t == 0:
                    off_copy[level].wait()
                if level == 3:
                    break
                to = NODE[level + 1] - 16 + t * (m // 2)

                def near(k, level=level, m=m, to=to):
                    value = product(t, m, level, 2 * k, 1) + product(t, m, level, 2 * k + 1, 1)
                    if level > 0:
                        value = value + waiting[to + k]
                    low_put(cb.at[t], k, value)

                each(m // 2, near)

                def far(level=level, m=m, above=above):
                    def one(j):
                        for a in range(2, above + 1):
                            k = NODE[level + a] - 16 + (t * m + j) // 2**a
                            waiting[k] = waiting[k] + product(t, m, level, j, a)

                    each(m, one, 2)

                for _ in col_reduce(t, m // 2, to * PITCH, far):
                    yield 1

        halves = [half(0), half(1)]
        for g in halves:
            next(g)
        for g in (2, 3):

            def others(h, j, v, g=g):
                rg[h, low_rows(8 * (g - 2) + j), :] = v

            unpack(g, gather_core(g, gathers[g]), 8 if g == 2 else 7, others)
        run(halves)
        low_put(cb.at[0], 0, waiting[14] + product(0, 1, 3, 0, 1) + product(1, 1, 3, 0, 1))
        run([col_steps(0, 1, 14 * PITCH)])
        inv_copy[4].wait()
        solve(0, 1, 4)
        run([row_steps(0, 1, 4, True)])

    pl.run_scoped(
        forward_sweep,
        pltpu.VMEM((K, LOW, TALL), BF),
        pltpu.VMEM((NOFF, LOW, TALL), BF),
        pltpu.VMEM((15, LOW, R), F32),
    )

    def backward_sweep(ui, uo, upward):
        spot = lax.broadcasted_iota(jnp.int32, (24, LOW), 1)
        at_row = lax.broadcasted_iota(jnp.int32, (24, LOW), 0) + col * SMALL
        own = jnp.where(spot == at_row, 1.0, 0.0).astype(BF)
        inv_copy, off_copy = {}, {}
        for level in reversed(range(LEVELS)):
            if level < 4:
                off_copy[level] = fetch(
                    uoff, uo, SLOT[level], SLOT[level + 1] - SLOT[level], 5 + level
                )
            inv_copy[level] = fetch(uinv, ui, NODE[level], MEMBERS[level], level)

        def solve(t, m, level):
            first = NODE[level] + t * m

            def one(j):
                low_put(cb.at[t], j, dot(ui[first + j], tall_get(xb.at[t], m, j)))

            each(m, one)

        def product(t, level, under, j, k):
            slot = SLOT[under] + j * (LEVELS - 1 - under) + level - under - 1
            scale = present[slot].astype(F32)
            return scale * dot_first(uo[slot], low_get(lowb.at[t], k))

        def show(t, m, level):
            for j in range(m):
                v = dot(own, low_get(lowb.at[t], j))[:SMALL]
                for h in (0, 1):
                    shown[h, pl.ds(NODE[level] - 16 + t * m + j, SMALL, stride=16), :] = v[
                        :, h * H : (h + 1) * H
                    ]

        inv_copy[4].wait()
        solve(0, 1, 4)
        run([col_steps(0, 1)])
        off_copy[3].wait()
        for t in (0, 1):
            tall_put(pb.at[t], 1, 0, product(0, 4, 3, t, 0))

        def half(t):
            for _ in row_reduce(t, 1, 3, False):
                yield 1
            for level in (3, 2, 1):
                m = MEMBERS[level] // 2
                if t == 0:
                    inv_copy[level].wait()
                solve(t, m, level)
                for _ in col_reduce(t, m):
                    yield 1

                def near(i, level=level, m=m):
                    j = t * 2 * m + i
                    value = product(t, level, level - 1, j, i // 2)
                    tall_put(pb.at[t], 2 * m, i, value + upward[NODE[level - 1] + j])

                each(2 * m, near)
                steps = row_reduce(t, 2 * m, level - 1, False)
                next(steps)
                yield 1
                for under in range(level - 2, -1, -1):

                    def far(i, level=level, m=m, under=under):
                        j = t * (MEMBERS[under] // 2) + i
                        value = product(t, level, under, j, i // 2 ** (level - under))
                        upward[NODE[under] + j] = value + upward[NODE[under] + j]

                    each(MEMBERS[under] // 2, far, 2)
                show(t, m, level)
                yield 1
                for _ in steps:
                    yield 1
            if t == 0:
                inv_copy[0].wait()
            for j in range(8):
                v = dot(ui[t * 8 + j], tall_get(xb.at[t], 8, j))
                for h in (0, 1):
                    wide[t, h, pl.ds(j, LOW, stride=8), :] = v[:, h * H : (h + 1) * H]
            first = []
            for h in (0, 1):
                for c in range(8):
                    v = wide[t, h, pl.ds(c * GROUP, GROUP), :]
                    sp[t, h, c // 2, c % 2, 0:GROUP, :] = v.astype(BF)
                first.append(
                    send(sp.at[t, h, :, 1 - core], crs.at[t, h], FC + t * 2 + h, sibling)
                )
            yield 1
            second = []
            for h in (0, 1):
                wait([first[h]])
                copies = []
                for d in (2, 1, 3):
                    to = (y + d) % 4
                    v = sp[t, h, to, core].astype(F32) + crs[t, h, to].astype(F32)
                    fys[t, h, to] = v.astype(BF)
                    copies.append(
                        send(
                            fys.at[t, h, to],
                            fyr.at[t, h, d - 1],
                            FY + t * 6 + h * 3 + d - 1,
                            ypeer(d),
                        )
                    )
                second.append(copies)
            yield 1
            if t == 0:
                for i in range(SMALL):
                    for h in (0, 1):
                        v = shown[h, pl.ds(i * 16, 16), :]
                        out[pl.ds(i * 32 + 16, 16), h * H : (h + 1) * H] = v
            for h in (0, 1):
                wait(second[h])
                v = sp[t, h, y, core].astype(F32) + crs[t, h, y].astype(F32)
                for k in range(3):
                    v = v + fyr[t, h, k].astype(F32)
                for i in range(SMALL):
                    out[pl.ds(i * 32 + t * 8, 8), h * H : (h + 1) * H] = v[8 * i : 8 * i + 8]

        halves = [half(0), half(1)]
        for g in halves:
            next(g)
        for h in (0, 1):
            topb[h, :, :] = lowb[0, h, 0:PITCH, :]

        def root_part(under, first, n):
            def one(i):
                j = first + i
                slot = SLOT[under] + j * (LEVELS - 1 - under) + 3 - under
                scale = present[slot].astype(F32)
                upward[NODE[under] + j] = scale * dot_first(uo[slot], low_get(topb, 0))

            each(n, one, 2)

        def root_far():
            for under in (2, 1, 0):
                off_copy[under].wait()
                for first in range(0, MEMBERS[under], 4):
                    root_part(under, first, 4)
                    if (under, first) != (0, 12):
                        if (under, first) != (0, 8):
                            yield 1
            yield 1

        show(0, 1, 4)
        run(halves + [root_far()])

    pl.run_scoped(
        backward_sweep,
        pltpu.VMEM((K, LOW, TALL), BF),
        pltpu.VMEM((NOFF, LOW, TALL), BF),
        pltpu.VMEM((30, TALL, R), F32),
    )


def on_device(right_sides, lower_inv, lower_off, upper_inv, upper_off, present):
    vmem = pl.BlockSpec(memory_space=pltpu.VMEM)
    hbm = pl.BlockSpec(memory_space=pl.ANY)
    out = pl.pallas_call(
        kernel,
        out_shape=jax.ShapeDtypeStruct((32 * SMALL, R), F32),
        in_specs=[vmem, pl.BlockSpec(memory_space=pltpu.SMEM), hbm, hbm, hbm, hbm],
        out_specs=vmem,
        scratch_shapes=[
            pltpu.VMEM((2, 2, 4, 608, H), BF),
            pltpu.VMEM((2, 2, 3, 608, H), BF),
            pltpu.VMEM((2, 2, 608, H), BF),
            pltpu.VMEM((2, 2, 3, 608, H), BF),
            pltpu.VMEM((2, 2, 4, 608, H), BF),
            pltpu.VMEM((2, 2, FWROWS, H), F32),
            pltpu.VMEM((2, 2, 608, H), F32),
            pltpu.VMEM((2, 2, 4 * PITCH, H), BF),
            pltpu.VMEM((2, 4 * PITCH, H), BF),
            pltpu.VMEM((2, 4 * PITCH, H), F32),
            pltpu.VMEM((2, 4 * PITCH, H), BF),
            pltpu.VMEM((2, 2, 3, 4 * PITCH, H), BF),
            pltpu.VMEM((2, 2, 8 * PITCH, H), BF),
            pltpu.VMEM((2, PITCH, H), BF),
            pltpu.VMEM((2, 15 * PITCH, H), BF),
            pltpu.VMEM((4, 2, 4, 2, PITCH, H), BF),
            pltpu.VMEM((2, 2, 8 * GROUP + 16, H), F32),
            pltpu.VMEM((2, 25 * 16, H), F32),
            pltpu.VMEM((2, 2, 4, 2, PITCH, H), BF),
            pltpu.VMEM((2, 2, 4, PITCH, H), BF),
            pltpu.VMEM((2, 2, 4, PITCH, H), BF),
            pltpu.VMEM((2, 2, 3, PITCH, H), BF),
            pltpu.SemaphoreType.DMA((NSEM,)),
            pltpu.SemaphoreType.DMA((NSEM,)),
            pltpu.SemaphoreType.DMA((9,)),
        ],
        compiler_params=pltpu.CompilerParams(
            collective_id=0, has_side_effects=True, vmem_limit_bytes=60 * 1024 * 1024
        ),
    )(
        jnp.swapaxes(right_sides, 0, 1),
        present,
        jnp.swapaxes(lower_inv, 1, 2),
        lower_off,
        upper_inv,
        jnp.swapaxes(upper_off, 1, 2),
    )
    return jnp.swapaxes(out.reshape(SMALL, 32, R)[:, :K], 0, 1)


def solution(mesh):
    placed = (
        P(None, ("row", "col"), None),
        P(None, "col", "row"),
        P(None, "row", "col"),
        P(None, "row", "col"),
        P(None, "col", "row"),
        P(),
    )
    return jax.shard_map(
        on_device,
        mesh=mesh,
        in_specs=placed,
        out_specs=P(None, ("row", "col"), None),
        check_vma=False,
    )
```
